256 devices in a mesh: loop: 16 (over x, y_lo, core), ep: 16 (over z, y_hi).
Axes of the slice: x: 4, y: 4 (y_hi: 2, y_lo: 2; y = y_hi * 2 + y_lo), z: 8, core: 2. Of those that a mesh axis runs over, the one named last changes fastest.
Arguments:
- tokens: bfloat16 [32768, 2048], P(('loop', 'ep')), may hold values from -6 to 6
- cotangent: bfloat16 [32768, 2048], P(('loop', 'ep')), may hold values from -6 to 6
- route_weight: float32 [32768, 2], P(('loop', 'ep')), may hold values from 0.1 to 1
- cold_ids: int32 [32768, 1], P(('loop', 'ep')), may hold values from 0 to 127; in each aligned block of 128 rows (0 to 127, 128 to 255, ...) at most 2 rows name the same one
- hot_pick: int32 [32768], P(('loop', 'ep')), may hold values 0 or 1
- hot_in: bfloat16 [768, 2, 2048], P('loop'), may hold values from -0.125 to 0.125
- hot_out: bfloat16 [768, 2048], P('loop'), may hold values from -0.21875 to 0.21875
- cold_in: bfloat16 [16, 16, 384, 2, 2048], P('loop', 'ep'), may hold values from -0.125 to 0.125
- cold_out: bfloat16 [16, 16, 384, 2048], P('loop', 'ep'), may hold values from -0.21875 to 0.21875
Outputs:
- moe_out: bfloat16 [32768, 2048], P(('loop', 'ep'))
- input_grad: bfloat16 [32768, 2048], P(('loop', 'ep'))
- hot_in_grad: bfloat16 [768, 2, 2048], P('loop')
- hot_out_grad: bfloat16 [768, 2048], P('loop')
- cold_in_grad: bfloat16 [16, 16, 384, 2, 2048], P('loop', 'ep')
- cold_out_grad: bfloat16 [16, 16, 384, 2048], P('loop', 'ep')
The draws below stay inside these ranges and needn't reach their ends.
Inputs may be any that keep to these rules, and one draw needn't show every extreme that they name: `cold_ids`: among the 128 tokens of one device, a cold expert is picked by at most 2 tokens, and some cold expert by exactly 2 on some device.
All inputs are finite; a program needn't handle non-finite values. No bound on the sum of `hot_pick` on one device may be relied on, other than what follows from the above.
Results may differ from the reference program's by a relative error of at most 0.03.
Values may be sent and summed in bfloat16 or wider, within the bound.
No kernel may reach another device: no remote copies, remote signals or barrier semaphores. Data moves between devices by JAX's collectives and lax.ppermute only.
A program may use at most 128 MiB of HBM per device.

```python
import math
import jax
import jax.numpy as jnp
import numpy as np
from jax import lax

D = 2048
FF = 768
TOK_DEV = 128
PICKS = 1
HALF = 384
PAIRS = 8
COLD = 128
CAP = 2
TOKENS = 32768
N_LOOP = 16
N_EP = 16


def set_ends(array, own_key, low, largest):
    extent = array.shape
    place = [jax.random.randint(jax.random.fold_in(own_key, axis), (), 0, extent[axis]) for axis in range(len(extent))]
    array = array.at[tuple(place)].set(low)
    longest = extent.index(max(extent))
    place[longest] = (place[longest] + 1) % extent[longest]
    return array.at[tuple(place)].set(largest)


def shard_levels(key, extent, cuts, least, high):
    loudness, own = 1.0, jax.random.fold_in(key, 6)
    for dim, parts in cuts:
        draws = jnp.exp(jax.random.uniform(jax.random.fold_in(own, dim), (parts,), jnp.float32, least / len(cuts), high / len(cuts)))
        loudness = loudness * jnp.repeat(draws, extent[dim] // parts).reshape([-1 if axis == dim else 1 for axis in range(len(extent))])
    return loudness


def deal_out(own_key, own, number, rows, count, top, limit, lean):
    order = jax.random.permutation(own_key, count)
    crowded, common = load_shares(count, rows * top, limit, lean, True), load_shares(count, rows * top, limit, lean, False)
    places = jnp.arange(count)

    def named(lengths, rotation):
        used = int((lengths > 0).sum())
        fixed = max(1, used // 4)
        moved = fixed + (places - fixed + rotation * (used - fixed)) % max(1, count - fixed)
        return jnp.zeros((count,), jnp.int32).at[order[jnp.where(places < fixed, places, moved)]].set(jnp.asarray(lengths, jnp.int32))

    lengths = jnp.where(number % 4 == 0, named(crowded, number // 4), named(common, number - number // 4 - 1))
    mixed = jax.random.permutation(jax.random.fold_in(own, 3), count)
    source_of, sink = mixed[0:count // 2 * 2:2], mixed[1:count // 2 * 2:2]
    margin = jnp.minimum(lengths[source_of] - 1, limit - lengths[sink]) // 2
    margin = jnp.where((source_of == order[0]) | (sink == order[0]) | (lengths[sink] == 0), 0, jnp.maximum(margin, 0))
    moved = jax.random.randint(jax.random.fold_in(own, 4), (count // 2,), 0, 1 << 20) % (margin + 1)
    lengths = lengths.at[source_of].add(-moved).at[sink].add(moved)
    items = jnp.searchsorted(jnp.cumsum(lengths), jnp.arange(rows * top), side="right").astype(jnp.int32)
    grid = items.reshape(top, rows).T
    grid = grid[jax.random.permutation(jax.random.fold_in(own, 1), rows)]
    rotation = jax.random.randint(jax.random.fold_in(own, 2), (rows, 1), 0, top)
    return jnp.take_along_axis(grid, (jnp.arange(top)[None, :] + rotation) % top, axis=1)


def load_shares(number_of, total, bound, lean, full):
    weights = [(1 << 20) // math.isqrt(standing ** lean) + 1 for standing in range(1, number_of + 1)]
    largest = bound if full else min(bound, max(-(-total // number_of), total * weights[0] // sum(weights)))
    least = 1 if total - largest >= number_of - 1 else 0
    given, spare = [largest] + [least] * (number_of - 1), total - largest - least * (number_of - 1)
    while spare > 0:
        free = [i for i in range(1, number_of) if given[i] < largest] or [i for i in range(1, number_of) if given[i] < bound]
        whole, remaining = sum([weights[i] for i in free]), spare
        for i in free:
            extra = min(bound - given[i], max(1, remaining * weights[i] // whole), spare)
            given[i] = given[i] + extra
            spare = spare - extra
    return np.array(given)


def normal_values(rng, shape, scale, reach, shards=(), kind=jnp.bfloat16):
    entries = scale * jax.random.normal(rng, shape, jnp.float32)
    if shards:
        entries = entries * shard_levels(rng, shape, shards, -0.22, 0.18)
    return jnp.clip(entries, -reach, reach).astype(kind)


def setup_inputs(seed: int = 0) -> dict:
    key_list = jax.random.split(jax.random.key(seed), 10)
    tokens = normal_values(key_list[0], (TOKENS, D), 1.0, 6.0, ((0, 256),))
    cotangent = normal_values(key_list[1], (TOKENS, D), 1.0, 6.0, ((0, 256),))
    route_weight = jnp.clip(jnp.exp(math.log(1.0) - 2.3025851 * jax.random.uniform(key_list[2], (TOKENS, PICKS + 1), jnp.float32) ** shard_levels(key_list[2], (TOKENS, PICKS + 1), ((0, 256),), -0.2, 0.2)), 0.1, 1.0)
    cold_ids_keys = jax.random.split(jax.random.fold_in(key_list[3], 1), TOKENS // TOK_DEV)
    cold_ids_turns = jax.random.permutation(jax.random.fold_in(key_list[3], 3), TOKENS // TOK_DEV)
    cold_ids = jax.vmap(lambda own, number: deal_out(jax.random.fold_in(key_list[3], 2), own, number, TOK_DEV, COLD, PICKS, CAP, 2))(cold_ids_keys, cold_ids_turns).reshape((TOKENS, PICKS))
    hot_pick = set_ends((jax.random.randint(key_list[4], (TOKENS,), 0, 4) < 3).astype(jnp.int32), jax.random.fold_in(key_list[4], 1), 0, 1)
    hot_in = normal_values(key_list[5], (FF, 2, D), D ** -0.5, 0.125, ((0, 16),))
    hot_out = normal_values(key_list[6], (FF, D), FF ** -0.5, 0.21875, ((0, 16),))
    cold_in = normal_values(key_list[7], (N_LOOP, N_EP, HALF, 2, D), D ** -0.5, 0.125, ((0, 16), (1, 16)))
    cold_out = normal_values(key_list[8], (N_LOOP, N_EP, HALF, D), FF ** -0.5, 0.21875, ((0, 16), (1, 16)))
    return {"tokens": tokens, "cotangent": cotangent, "route_weight": route_weight, "cold_ids": cold_ids, "hot_pick": hot_pick, "hot_in": hot_in, "hot_out": hot_out, "cold_in": cold_in, "cold_out": cold_out}


def forward_half(row_block, weight_in, weight_out):
    dims = (((1,), (1,)), ((), ()))
    gate_proj = lax.dot_general(row_block, weight_in[:, 0, :], dims, preferred_element_type=jnp.float32)
    up_proj = lax.dot_general(row_block, weight_in[:, 1, :], dims, preferred_element_type=jnp.float32)
    active = gate_proj * jax.nn.sigmoid(gate_proj)
    hidden = (active * up_proj).astype(jnp.bfloat16)
    result = jnp.dot(hidden, weight_out, preferred_element_type=jnp.float32)
    return gate_proj, up_proj, hidden, result


def backward_half(grad_rows, weight_in, weight_out, gate_proj, up_proj):
    dims = (((1,), (1,)), ((), ()))
    sigmoid_part = jax.nn.sigmoid(gate_proj)
    active = gate_proj * sigmoid_part
    derivative = sigmoid_part * (1.0 + gate_proj * (1.0 - sigmoid_part))
    grad_hidden = lax.dot_general(grad_rows, weight_out, dims, preferred_element_type=jnp.float32)
    grad_gate = (grad_hidden * up_proj * derivative).astype(jnp.bfloat16)
    grad_up = (grad_hidden * active).astype(jnp.bfloat16)
    grad_input = jnp.dot(grad_gate, weight_in[:, 0, :], preferred_element_type=jnp.float32)
    grad_input = grad_input + jnp.dot(grad_up, weight_in[:, 1, :], preferred_element_type=jnp.float32)
    return grad_gate, grad_up, grad_input


def expert_grads(row_block, grad_rows, hidden, grad_gate, grad_up):
    dims = (((0,), (0,)), ((), ()))
    gate_grad = lax.dot_general(grad_gate, row_block, dims, preferred_element_type=jnp.float32)
    up_grad = lax.dot_general(grad_up, row_block, dims, preferred_element_type=jnp.float32)
    down_grad = lax.dot_general(hidden, grad_rows, dims, preferred_element_type=jnp.float32)
    return jnp.stack([gate_grad, up_grad], axis=1), down_grad


def reference(tokens, cotangent, route_weight, cold_ids, hot_pick, hot_in, hot_out, cold_in, cold_out):
    blocks = N_LOOP * N_EP
    rows_cap = blocks * CAP
    hot_scale = hot_pick.astype(jnp.float32) * route_weight[:, PICKS]
    hot_cot = (hot_scale[:, None] * cotangent.astype(jnp.float32)).astype(jnp.bfloat16)

    def hot_block(carried, block_pair):
        row_block, grad_rows = block_pair
        gate_proj, up_proj, hidden, result = forward_half(row_block, hot_in, hot_out)
        grad_gate, grad_up, grad_input = backward_half(grad_rows, hot_in, hot_out, gate_proj, up_proj)
        in_grads, down_grad = expert_grads(row_block, grad_rows, hidden, grad_gate, grad_up)
        term_rows = jnp.concatenate([in_grads, down_grad[:, None, :]], axis=1)
        rounded = lax.optimization_barrier(term_rows.astype(jnp.bfloat16)).astype(jnp.float32)
        return carried + rounded, (result, grad_input)

    hot_sum, (hot_y, hot_dx) = lax.scan(
        hot_block, jnp.zeros((FF, 3, D), jnp.float32),
        (tokens.reshape(blocks, TOK_DEV, D), hot_cot.reshape(blocks, TOK_DEV, D)))
    hot_y = hot_y.reshape(TOKENS, D)
    hot_dx = hot_dx.reshape(TOKENS, D)

    pick_total = TOK_DEV * PICKS
    flat_ids = cold_ids.reshape(blocks, pick_total)
    onehot = (flat_ids[:, :, None] == jnp.arange(COLD, dtype=jnp.int32)[None, None, :]).astype(jnp.int32)
    slot_index = jnp.sum(jnp.cumsum(onehot, axis=1) * onehot, axis=2) - 1
    device_index = jnp.arange(blocks, dtype=jnp.int32)[:, None]
    location = flat_ids * rows_cap + device_index * CAP + slot_index
    slot_table = jnp.full((COLD * rows_cap,), -1, jnp.int32).at[location.reshape(-1)].set(
        jnp.arange(blocks * pick_total, dtype=jnp.int32))
    weights_flat = route_weight[:, :PICKS].reshape(-1)

    def cold_expert(carried, expert):
        y_acc, dx_acc = carried
        slot_source = lax.dynamic_slice_in_dim(slot_table, expert * rows_cap, rows_cap)
        present = slot_source >= 0
        clamped = jnp.maximum(slot_source, 0)
        token_of = clamped // PICKS
        row_block = jnp.where(present[:, None], tokens[token_of], jnp.zeros((), jnp.bfloat16))
        pick_weight = jnp.where(present, weights_flat[clamped], jnp.float32(0.0))
        grad_rows = (pick_weight[:, None] * cotangent[token_of].astype(jnp.float32)).astype(jnp.bfloat16)
        pair_index = expert // N_EP
        column = expert % N_EP
        results = []
        inputs_back = []
        grads_in = []
        grads_out = []
        for half_index in range(2):
            weight_in = cold_in[2 * pair_index + half_index, column]
            weight_out = cold_out[2 * pair_index + half_index, column]
            gate_proj, up_proj, hidden, result = forward_half(row_block, weight_in, weight_out)
            grad_gate, grad_up, grad_input = backward_half(grad_rows, weight_in, weight_out, gate_proj, up_proj)
            in_grads, down_grad = expert_grads(row_block, grad_rows, hidden, grad_gate, grad_up)
            results.append(lax.optimization_barrier(result.astype(jnp.bfloat16)).astype(jnp.float32))
            inputs_back.append(lax.optimization_barrier(grad_input.astype(jnp.bfloat16)).astype(jnp.float32))
            grads_in.append(in_grads.astype(jnp.bfloat16))
            grads_out.append(down_grad.astype(jnp.bfloat16))
        pick_out = lax.optimization_barrier((results[0] + results[1]).astype(jnp.bfloat16)).astype(jnp.float32)
        pick_dx = lax.optimization_barrier((inputs_back[0] + inputs_back[1]).astype(jnp.bfloat16)).astype(jnp.float32)
        y_acc = y_acc.at[token_of].add(pick_weight[:, None] * pick_out)
        dx_acc = dx_acc.at[token_of].add(jnp.where(present[:, None], pick_dx, jnp.float32(0.0)))
        return (y_acc, dx_acc), (jnp.stack(grads_in), jnp.stack(grads_out))

    (cold_y, cold_dx), (gin_all, gout_all) = lax.scan(
        cold_expert, (jnp.zeros((TOKENS, D), jnp.float32), jnp.zeros((TOKENS, D), jnp.float32)),
        jnp.arange(COLD, dtype=jnp.int32))
    cold_in_grad = gin_all.reshape(PAIRS, N_EP, 2, HALF, 2, D).transpose(0, 2, 1, 3, 4, 5).reshape(N_LOOP, N_EP, HALF, 2, D)
    cold_out_grad = gout_all.reshape(PAIRS, N_EP, 2, HALF, D).transpose(0, 2, 1, 3, 4).reshape(N_LOOP, N_EP, HALF, D)
    moe_out = (hot_scale[:, None] * hot_y + cold_y).astype(jnp.bfloat16)
    input_grad = (hot_dx + cold_dx).astype(jnp.bfloat16)
    hot_total = hot_sum.astype(jnp.bfloat16)
    return moe_out, input_grad, hot_total[:, :2, :], hot_total[:, 2, :], cold_in_grad, cold_out_grad
```

```python
import functools

import jax
import jax.numpy as jnp
from jax import lax
from jax.experimental import pallas as pl
from jax.experimental.pallas import tpu as pltpu
from jax.sharding import Mesh
from jax.sharding import PartitionSpec as P

BF = jnp.bfloat16
F32 = jnp.float32
NT = (((1,), (1,)), ((), ()))
TN = (((0,), (0,)), ((), ()))
EVERY = ("x", "l", "c", "z", "h")
EXPERTS = ("x", "l", "z", "h")


def dot(a, b, dims=(((1,), (0,)), ((), ()))):
    return lax.dot_general(a, b, dims, preferred_element_type=F32)


def call(kernel, outs, scratch, flops, name, *args):
    moved = sum(a.size * a.dtype.itemsize for a in args)
    moved += sum(o.size * o.dtype.itemsize for o in outs)
    return pl.pallas_call(
        kernel,
        out_shape=outs,
        in_specs=[pl.BlockSpec(memory_space=pltpu.VMEM)] * len(args),
        out_specs=[pl.BlockSpec(memory_space=pltpu.VMEM)] * len(outs),
        scratch_shapes=scratch,
        compiler_params=pltpu.CompilerParams(vmem_limit_bytes=24 << 20),
        cost_estimate=pl.CostEstimate(flops=flops, bytes_accessed=moved, transcendentals=0),
        name=name,
    )(*args)


def shape(*dims):
    return jax.ShapeDtypeStruct(dims, BF)


def as_row(column, eye):
    return jnp.sum(jnp.where(eye, column, 0), axis=0, keepdims=True)


def as_column(row, eye):
    return jnp.sum(jnp.where(eye, row, 0), axis=1, keepdims=True)


def send_kernel(tok, cot, rw, ids, pick, packed, hot_a, hot_b, stack):
    rows, width = tok.shape
    half = width // 2
    up, across = (lax.broadcasted_iota(jnp.int32, (rows, rows), d) for d in (0, 1))
    eye = up == across
    id_col = jnp.broadcast_to(ids[...], (rows, rows))
    id_row = as_row(id_col, eye)
    slot_row = jnp.sum(
        jnp.where((id_col == id_row) & (up < across), 1, 0), axis=0, keepdims=True
    )
    place = 8 * id_row + 2 * slot_row
    cotangent = cot[...].astype(F32)
    cold_cot = (rw[:, 0:1] * cotangent).astype(BF)
    scale = as_column(pick[...].astype(F32), eye) * rw[:, 1:2]
    hot_cot = (scale * cotangent).astype(BF)
    mid = rows // 2
    hot_a[0:mid] = tok[0:mid]
    hot_a[mid:rows] = hot_cot[0:mid]
    hot_b[0:mid] = tok[mid:rows]
    hot_b[mid:rows] = hot_cot[mid:rows]
    stack[0:rows] = tok[:, 0:half]
    stack[rows : 2 * rows] = tok[:, half:width]
    stack[2 * rows : 3 * rows] = cold_cot[:, 0:half]
    stack[3 * rows : 4 * rows] = cold_cot[:, half:width]
    step = 256
    for first in range(0, packed.shape[0], step):
        at = first + lax.broadcasted_iota(jnp.int32, (step, rows), 0) - place
        pick_rows = jnp.concatenate(
            [jnp.where(at == 4 * k + f, 1.0, 0.0).astype(BF) for k in (0, 1) for f in (0, 1)], axis=1
        )
        packed[first : first + step] = dot(pick_rows, stack[...]).astype(BF)


def order(n, transposed):
    packed_at, plain_at = (
        lax.broadcasted_iota(jnp.int32, (n, n), d) for d in ((0, 1) if transposed else (1, 0))
    )
    sender, place = packed_at >> 3, packed_at & 7
    group = 2 * (place >> 2) + (place & 1)
    target = group * (n // 4) + 2 * sender + ((place >> 1) & 1)
    return jnp.where(plain_at == target, 1.0, 0.0).astype(BF)


def gated(g, u, dh):
    s = jax.nn.sigmoid(g)
    act = g * s
    h = (act * u).astype(BF)
    dg = (dh * u * (s * (1.0 + g * (1.0 - s)))).astype(BF)
    du = (dh * act).astype(BF)
    return h, dg, du


def cold_kernel(packed, wg, wu, wd, back, x, c, h_out, dg_out, du_out):
    n = 256
    quarter = n // 4
    half = packed.shape[1]
    sort = order(n, False)
    for j in range(packed.shape[0] // n):
        t = dot(sort, packed[n * j : n * j + n]).astype(BF)
        r = slice(quarter * j, quarter * j + quarter)
        x[r, 0:half] = t[0:quarter]
        x[r, half:] = t[quarter : 2 * quarter]
        c[r, 0:half] = t[2 * quarter : 3 * quarter]
        c[r, half:] = t[3 * quarter :]
    g = dot(x[...], wg[...], NT)
    u = dot(x[...], wu[...], NT)
    dh = dot(c[...], wd[...], NT)
    h, dg, du = gated(g, u, dh)
    h_out[...] = h
    dg_out[...] = dg
    du_out[...] = du
    unsort = order(n, True)
    o = dot(h, wd[...]).astype(BF)
    dx = (dot(dg, wg[...]) + dot(du, wu[...])).astype(BF)
    for j in range(packed.shape[0] // n):
        r = slice(quarter * j, quarter * j + quarter)
        t = jnp.concatenate([o[r, 0:half], o[r, half:], dx[r, 0:half], dx[r, half:]], axis=0)
        back[n * j : n * j + n] = dot(unsort, t).astype(BF)


def cold_grad_kernel(xa, ca, ha, ga, ua, xb, cb, hb, gb, ub, gate, up, down):
    gate[...] = (dot(ga[...], xa[...], TN) + dot(gb[...], xb[...], TN)).astype(BF)
    up[...] = (dot(ua[...], xa[...], TN) + dot(ub[...], xb[...], TN)).astype(BF)
    down[...] = (dot(ha[...], ca[...], TN) + dot(hb[...], cb[...], TN)).astype(BF)


def hot_kernel(*refs):
    parts, blocks = refs[0:8], refs[8:13]
    own, near, away = refs[13:16]
    grads = refs[16:20]
    x, c, w_in, w_out = refs[20:24]
    mid = parts[0].shape[0] // 2
    for i, part in enumerate(parts):
        x[mid * i : mid * i + mid] = part[0:mid]
        c[mid * i : mid * i + mid] = part[mid:]
    units = blocks[0].shape[0] // 3
    count = 4 * units
    cut = blocks[3].shape[0]

    def rows_of(block, lo, hi):
        if block < 3:
            return [(0, blocks[block], lo, hi)]
        found = []
        if lo < cut:
            found.append((0, blocks[3], lo, min(hi, cut)))
        if hi > cut:
            found.append((max(cut - lo, 0), blocks[4], max(lo, cut) - cut, hi - cut))
        return found

    for b in range(4):
        for kind in range(3):
            target, base = (w_out, units * b) if kind == 2 else (w_in, count * kind + units * b)
            for at, ref, lo, hi in rows_of(b, units * kind, units * kind + units):
                target[base + at : base + at + hi - lo] = ref[lo:hi]
    hs, ds = [], []
    step = 256
    for first in range(0, x.shape[0], step):
        r = slice(first, first + step)
        gu = dot(x[r], w_in[...], NT)
        dh = dot(c[r], w_out[...], NT)
        h, dg, du = gated(gu[:, 0:count], gu[:, count:], dh)
        d = jnp.concatenate([dg, du], axis=1)
        o = dot(h, w_out[...]).astype(BF)
        dx = dot(d, w_in[...]).astype(BF)
        hs.append(h)
        ds.append(d)
        for i in range(step // mid):
            part = first // mid + i
            s = slice(mid * i, mid * i + mid)
            ref, at = ((own, 0), (away, 0), (near, 0), (away, 256))[part // 2]
            at = at + 2 * mid * (part % 2)
            ref[at : at + mid] = o[s]
            ref[at + mid : at + 2 * mid] = dx[s]
    h, d = jnp.concatenate(hs, axis=0), jnp.concatenate(ds, axis=0)
    in_grad = dot(d, x[...], TN).astype(BF)
    out_grad = dot(h, c[...], TN).astype(BF)
    for b in range(4):
        u = units * b
        grads[b][0:units] = in_grad[u : u + units]
        grads[b][units : 2 * units] = in_grad[count + u : count + u + units]
        grads[b][2 * units :] = out_grad[u : u + units]


def end_kernel(packed, own, sibling, side_a, side_b, rw, ids, pick, moe, grad):
    rows, width = moe.shape
    half = width // 2
    up, across = (lax.broadcasted_iota(jnp.int32, (rows, rows), d) for d in (0, 1))
    eye = up == across
    id_col = jnp.broadcast_to(ids[...], (rows, rows))
    id_row = as_row(id_col, eye)
    slot = jnp.sum(jnp.where((id_col == id_row) & (across < up), 1, 0), axis=1, keepdims=True)
    place = 8 * ids[...] + 2 * slot
    at = lax.broadcasted_iota(jnp.int32, (rows, packed.shape[0]), 1) - place
    scale = as_column(pick[...].astype(F32), eye) * rw[:, 1:2]
    weight = rw[:, 0:1]
    mid = rows // 2
    for k in (0, 1):
        for f in (0, 1):
            chosen = jnp.where(at == 4 * k + f, 1.0, 0.0).astype(BF)
            cold = dot(chosen, packed[...])
            cols = slice(half * f, half * f + half)
            for i, side in ((0, side_a), (1, side_b)):
                s = slice(mid * k, mid * k + mid)
                b = slice(rows * i + mid * k, rows * i + mid * k + mid)
                t = slice(mid * i, mid * i + mid)
                hot = own[b, cols].astype(F32) + sibling[b, cols].astype(F32) + side[s, cols].astype(F32)
                if k == 0:
                    moe[t, cols] = (scale[t] * hot + weight[t] * cold[t]).astype(BF)
                else:
                    grad[t, cols] = (hot + cold[t]).astype(BF)


def per_device(tokens, cotangent, route_weight, cold_ids, hot_pick, hot_in, hot_out, cold_in, cold_out):
    rows, width = tokens.shape
    sizes = {name: lax.axis_size(name) for name in EVERY}
    nx, nz = sizes["x"], sizes["z"]
    units = hot_out.shape[0]
    experts = nx * sizes["l"] * nz * sizes["h"]
    cut = 80

    def along_x(value, step):
        return lax.ppermute(value, "x", [(i, (i + step) % nx) for i in range(nx)])

    def along_y(value, step):
        def index(y):
            return (y % 2) * 2 + y // 2

        return lax.ppermute(value, ("l", "h"), [(index(y), index((y + step) % 4)) for y in range(4)])

    def sibling(value):
        return lax.ppermute(value, "c", [(0, 1), (1, 0)])

    def exchange(value):
        return lax.all_to_all(value, EXPERTS, split_axis=0, concat_axis=0, tiled=True)

    pick_row = hot_pick.reshape(1, rows)
    packed, hot_a, hot_b = call(
        send_kernel,
        [shape(experts * 8, width // 2), shape(rows, width), shape(rows, width)],
        [pltpu.VMEM((4 * rows, width // 2), BF)],
        2 * experts * 8 * 4 * rows * width // 2,
        "send",
        tokens, cotangent, route_weight, cold_ids, pick_row,
    )
    block = jnp.concatenate([hot_in[:, 0], hot_in[:, 1], hot_out], axis=0)
    from_left, from_right = along_x(block, 1), along_x(block, -1)
    far_a, far_b = along_x(from_left[:cut], 1), along_x(from_right[cut:], -1)
    side_a, side_b = along_y(hot_a, 1), along_y(hot_b, -1)
    parts = [hot_a, hot_b, sibling(hot_a), sibling(hot_b), side_a, side_b, sibling(side_a), sibling(side_b)]

    got = exchange(packed)

    own, near, away, grad_own, grad_left, grad_right, grad_far = call(
        hot_kernel,
        [shape(2 * rows, width), shape(2 * rows, width), shape(4 * rows, width)] + [shape(3 * units, width)] * 4,
        [
            pltpu.VMEM((4 * rows, width), BF),
            pltpu.VMEM((4 * rows, width), BF),
            pltpu.VMEM((8 * units, width), BF),
            pltpu.VMEM((4 * units, width), BF),
        ],
        9 * 2 * 4 * rows * 4 * units * width,
        "hot",
        *parts, block, from_left, from_right, far_a, far_b,
    )
    away = sibling(away)
    summed = near.astype(F32) + away[2 * rows :].astype(F32)
    summed = summed.astype(BF)
    hot_side_a, hot_side_b = along_y(summed[:rows], -1), along_y(summed[rows:], 1)
    got_a, got_b = along_x(grad_far[:cut], 1), along_x(grad_far[cut:], -1)
    to_right = jnp.concatenate(
        [(grad_right[:cut].astype(F32) + got_a.astype(F32)).astype(BF), grad_right[cut:]], axis=0
    )
    to_left = jnp.concatenate(
        [grad_left[:cut], (grad_left[cut:].astype(F32) + got_b.astype(F32)).astype(BF)], axis=0
    )
    got_right, got_left = along_x(to_right, 1), along_x(to_left, -1)
    total = (grad_own.astype(F32) + got_right.astype(F32) + got_left.astype(F32)).astype(BF)
    z = lax.axis_index("z")
    steps = [("h", 1, lax.axis_index("h"))]
    steps += [("z", 1, z & 1), ("z", 2, (z >> 1) & 1), ("z", 4, z >> 2)]
    for name, flip, bit in steps:
        part = total.shape[1] // 2
        pairs = [(i, i ^ flip) for i in range(sizes[name])]
        sent = lax.dynamic_slice_in_dim(total, (1 - bit) * part, part, axis=1)
        kept = lax.dynamic_slice_in_dim(total, bit * part, part, axis=1)
        came = lax.ppermute(sent, name, pairs)
        total = (kept.astype(F32) + came.astype(F32)).astype(BF)
    for name, flip, bit in reversed(steps):
        pairs = [(i, i ^ flip) for i in range(sizes[name])]
        came = lax.ppermute(total, name, pairs)
        total = jnp.where(
            bit == 0, jnp.concatenate([total, came], axis=1), jnp.concatenate([came, total], axis=1)
        )

    half_units = cold_out.shape[2]
    gate, up, down = cold_in[0, 0, :, 0], cold_in[0, 0, :, 1], cold_out[0, 0]

    def cold(received):
        picked = 2 * experts
        return call(
            cold_kernel,
            [shape(*received.shape)]
            + [shape(picked, width)] * 2
            + [shape(picked, half_units)] * 3,
            [],
            6 * 2 * picked * half_units * width,
            "cold",
            received, gate, up, down,
        )

    theirs = sibling(got)
    mine_back, *mine = cold(got)
    their_back, *their = cold(theirs)
    came_back = sibling(their_back)
    back = (mine_back.astype(F32) + came_back.astype(F32)).astype(BF)
    returned = exchange(back)
    gate_grad, up_grad, down_grad = call(
        cold_grad_kernel,
        [shape(half_units, width)] * 3,
        [],
        3 * 2 * 4 * experts * half_units * width,
        "cold_grad",
        *mine, *their,
    )
    cold_in_grad = jnp.stack([gate_grad, up_grad], axis=1)[None, None]
    cold_out_grad = down_grad[None, None]

    moe_out, input_grad = call(
        end_kernel,
        [shape(rows, width), shape(rows, width)],
        [],
        2 * 4 * rows * 8 * experts * width // 2,
        "end",
        returned, own, away[: 2 * rows], hot_side_a, hot_side_b, route_weight, cold_ids, pick_row,
    )
    hot_in_grad = jnp.stack([total[:units], total[units : 2 * units]], axis=1)
    return moe_out, input_grad, hot_in_grad, total[2 * units :], cold_in_grad, cold_out_grad


def solution(mesh):
    fine = Mesh(mesh.devices.reshape(4, 2, 2, 8, 2), EVERY)
    loop, ep = ("x", "l", "c"), ("z", "h")
    tokens = P(EVERY, None)
    return jax.shard_map(
        per_device,
        mesh=fine,
        in_specs=(
            tokens, tokens, tokens, tokens, P(EVERY),
            P(loop, None, None), P(loop, None),
            P(loop, ep, None, None, None), P(loop, ep, None, None),
        ),
        out_specs=(
            tokens, tokens,
            P(loop, None, None), P(loop, None),
            P(loop, ep, None, None, None), P(loop, ep, None, None),
        ),
        check_vma=False,
    )
```

```python
import functools

import jax
import jax.numpy as jnp
from jax import lax
from jax.experimental import pallas as pl
from jax.experimental.pallas import tpu as pltpu
from jax.sharding import Mesh
from jax.sharding import PartitionSpec as P

BF = jnp.bfloat16
F32 = jnp.float32
NT = (((1,), (1,)), ((), ()))
TN = (((0,), (0,)), ((), ()))
EVERY = ("x", "l", "c", "z", "h")
EXPERTS = ("x", "l", "z", "h")


def dot(a, b, dims=(((1,), (0,)), ((), ()))):
    return lax.dot_general(a, b, dims, preferred_element_type=F32)


class Arriving:
    def __init__(self, source, target, semaphores, first, parts):
        self.target, self.rows = target, source.shape[0] // parts
        self.copies = [
            pltpu.make_async_copy(
                source.at[pl.ds(self.rows * i, self.rows)],
                target.at[pl.ds(self.rows * i, self.rows)],
                semaphores.at[first + i],
            )
            for i in range(parts)
        ]
        for copy in self.copies:
            copy.start()

    def get(self, upto=None):
        upto = self.target.shape[0] if upto is None else upto
        for i, copy in enumerate(self.copies):
            if copy is not None and self.rows * i < upto:
                copy.wait()
                self.copies[i] = None
        return self.target


def call(kernel, outs, scratch, flops, name, *args, after=()):
    moved = sum(a.size * a.dtype.itemsize for a in args)
    moved += sum(o.size * o.dtype.itemsize for o in outs)
    moved = moved if flops else 0
    n, m, skip, most = len(args), len(outs), len(after), 16
    parts = [4 if a.shape[0] == 1024 else 1 for a in args]

    def body(*refs):
        given, made = refs[:n], refs[n + skip : n + skip + m]
        held = refs[n + skip + m :]
        held_in, held_out, more = held[:n], held[n : n + m], held[n + m : -2]
        in_sem, out_sem = held[-2:]
        ins = [Arriving(given[i], held_in[i], in_sem, sum(parts[:i]), parts[i]) for i in range(n)]
        sent, begun = [], set()

        def send(i, lo=0, hi=None):
            begun.add(i)
            r = pl.ds(lo, (made[i].shape[0] if hi is None else hi) - lo)
            copy = pltpu.make_async_copy(held_out[i].at[r], made[i].at[r], out_sem.at[len(sent)])
            copy.start()
            sent.append(copy)

        kernel(ins, held_out, send, *more)
        for i in ins:
            i.get()
        for i in range(m):
            if i not in begun:
                send(i)
        for copy in sent:
            copy.wait()

    return pl.pallas_call(
        body,
        out_shape=outs,
        in_specs=[pl.BlockSpec(memory_space=pl.ANY)] * (n + skip),
        out_specs=[pl.BlockSpec(memory_space=pl.ANY)] * m,
        scratch_shapes=[pltpu.VMEM(a.shape, a.dtype) for a in args]
        + [pltpu.VMEM(o.shape, o.dtype) for o in outs]
        + list(scratch)
        + [pltpu.SemaphoreType.DMA((sum(parts),)), pltpu.SemaphoreType.DMA((most,))],
        compiler_params=pltpu.CompilerParams(vmem_limit_bytes=56 << 20),
        cost_estimate=pl.CostEstimate(flops=flops, bytes_accessed=moved, transcendentals=0),
        name=name,
    )(*args, *after)


def gate(value, *after):
    outside = pl.BlockSpec(memory_space=pl.ANY)
    return pl.pallas_call(
        lambda *refs: None,
        out_shape=jax.ShapeDtypeStruct(value.shape, value.dtype),
        in_specs=[outside] * (1 + len(after)),
        out_specs=outside,
        input_output_aliases={0: 0},
        name="gate",
    )(value, *after)


def shape(*dims):
    return jax.ShapeDtypeStruct(dims, BF)


def as_column(row, eye):
    return jnp.sum(jnp.where(eye, row, 0), axis=1, keepdims=True)


def eye_of(rows):
    up, across = (lax.broadcasted_iota(jnp.int32, (rows, rows), d) for d in (0, 1))
    return up == across


def rows_kernel(ins, outs, send):
    tok, cot, rw, pick = ins
    hot_a, hot_b = outs
    rows = hot_a.shape[0]
    mid = rows // 2
    tok = tok.get()
    hot_a[0:mid] = tok[0:mid]
    hot_b[0:mid] = tok[mid:rows]
    scale = as_column(pick.get()[...].astype(F32) * rw.get()[1:2], eye_of(rows))
    hot_cot = (scale * cot.get()[...].astype(F32)).astype(BF)
    hot_a[mid:rows] = hot_cot[0:mid]
    send(0)
    hot_b[mid:rows] = hot_cot[mid:rows]


def send_kernel(ins, outs, send, stack):
    tok, cot, rw, ids = [i.get() for i in ins]
    [packed] = outs
    rows, width = tok.shape
    half = width // 2
    up, across = (lax.broadcasted_iota(jnp.int32, (rows, rows), d) for d in (0, 1))
    eye = up == across
    id_row = jnp.broadcast_to(ids[...], (rows, rows))
    id_col = as_column(id_row, eye)
    slot_row = jnp.sum(
        jnp.where((id_col == id_row) & (up < across), 1, 0), axis=0, keepdims=True
    )
    place = 8 * ids[...] + 2 * slot_row
    cold_cot = (as_column(rw[0:1], eye) * cot[...].astype(F32)).astype(BF)
    stack[0:rows] = tok[:, 0:half]
    stack[rows : 2 * rows] = tok[:, half:width]
    stack[2 * rows : 3 * rows] = cold_cot[:, 0:half]
    stack[3 * rows : 4 * rows] = cold_cot[:, half:width]
    step = 256
    for first in range(0, packed.shape[0], step):
        at = first + lax.broadcasted_iota(jnp.int32, (step, rows), 0) - place
        pick_rows = jnp.concatenate(
            [jnp.where(at == 4 * k + f, 1.0, 0.0).astype(BF) for k in (0, 1) for f in (0, 1)], axis=1
        )
        packed[first : first + step] = dot(pick_rows, stack[...]).astype(BF)
        send(0, first, first + step)


def order(n, transposed):
    packed_at, plain_at = (
        lax.broadcasted_iota(jnp.int32, (n, n), d) for d in ((0, 1) if transposed else (1, 0))
    )
    sender, place = packed_at >> 3, packed_at & 7
    group = 2 * (place >> 2) + (place & 1)
    target = group * (n // 4) + 2 * sender + ((place >> 1) & 1)
    return jnp.where(plain_at == target, 1.0, 0.0).astype(BF)


def gated(g, u, dh):
    s = jax.nn.sigmoid(g)
    act = g * s
    h = (act * u).astype(BF)
    dg = (dh * u * (s * (1.0 + g * (1.0 - s)))).astype(BF)
    du = (dh * act).astype(BF)
    return h, dg, du


def unpack(packed, sort, x, c, first):
    n = sort.shape[0]
    quarter, half = n // 4, packed.target.shape[1]
    for j in range(packed.target.shape[0] // n):
        t = dot(sort, packed.get(n * j + n)[n * j : n * j + n]).astype(BF)
        r = slice(first + quarter * j, first + quarter * j + quarter)
        x[r, 0:half] = t[0:quarter]
        x[r, half:] = t[quarter : 2 * quarter]
        c[r, 0:half] = t[2 * quarter : 3 * quarter]
        c[r, half:] = t[3 * quarter :]


def cold_kernel(ins, outs, send, x, c):
    packed, wg, wu, wd = ins
    back, h_out, dg_out, du_out = outs
    n = 256
    quarter, half = n // 4, back.shape[1]
    unpack(packed, order(n, False), x, c, 0)
    wg = wg.get()
    g = dot(x[...], wg[...], NT)
    wu = wu.get()
    u = dot(x[...], wu[...], NT)
    wd = wd.get()
    dh = dot(c[...], wd[...], NT)
    h, dg, du = gated(g, u, dh)
    h_out[...] = h
    dg_out[...] = dg
    du_out[...] = du
    for i in (1, 2, 3):
        send(i)
    unsort = order(n, True)
    o = dot(h, wd[...]).astype(BF)
    dx = (dot(dg, wg[...]) + dot(du, wu[...])).astype(BF)
    for j in range(back.shape[0] // n):
        r = slice(quarter * j, quarter * j + quarter)
        t = jnp.concatenate([o[r, 0:half], o[r, half:], dx[r, 0:half], dx[r, half:]], axis=0)
        back[n * j : n * j + n] = dot(unsort, t).astype(BF)
        send(0, n * j, n * j + n)


def add_kernel(ins, outs, send):
    step = outs[0].shape[0] // 4
    for first in range(0, outs[0].shape[0], step):
        r = slice(first, first + step)
        outs[0][r] = sum(i.get(first + step)[r].astype(F32) for i in ins).astype(BF)
        send(0, first, first + step)


def mix_kernel(ins, outs, send):
    right, left, more_right, more_left = [i.get() for i in ins]
    part = more_right.shape[0]
    outs[0][0:part] = (right[0:part].astype(F32) + more_right[...].astype(F32)).astype(BF)
    outs[0][part:] = right[part:]
    send(0)
    outs[1][0:part] = left[0:part]
    outs[1][part:] = (left[part:].astype(F32) + more_left[...].astype(F32)).astype(BF)


def share_kernel(ins, outs, send):
    shares = ins[0].get()
    count = 8
    rows = shares.shape[0] // count
    total = sum(shares[rows * i : rows * i + rows].astype(F32) for i in range(count)).astype(BF)
    for i in range(count):
        outs[0][rows * i : rows * i + rows] = total


def weave(rows):
    row, column = (lax.broadcasted_iota(jnp.int32, (rows, rows), d) for d in (0, 1))
    return jnp.where(column == (row >> 1) + rows // 2 * (row & 1), 1.0, 0.0).astype(BF)


def assemble_kernel(ins, outs, send):
    mine, other, h = [i.get() for i in ins]
    inner, outer = outs
    units, width = outer.shape
    piece = mine.shape[1]
    count = mine.shape[0] // (3 * units)
    low = h[0:1] == 0
    order_of = weave(2 * units)
    for p in range(2 * count):
        at = 3 * units * (p % count)
        r = slice(at, at + 3 * units)
        a, b = mine[r].astype(F32), other[r].astype(F32)
        rows = jnp.where(low == (p < count), a, b).astype(BF)
        cols = slice(piece * p, piece * p + piece)
        inner[:, cols] = dot(order_of, rows[0 : 2 * units]).astype(BF)
        outer[:, cols] = rows[2 * units :]


def cold_grad_kernel(ins, outs, send, x, c):
    mine, theirs, ha, ga, ua, hb, gb, ub = ins
    sort = order(256, False)
    half = x.shape[0] // 2
    unpack(mine, sort, x, c, 0)
    unpack(theirs, sort, x, c, half)
    both = []
    for i, (a, b, rows) in enumerate(((ha, hb, c), (ga, gb, x), (ua, ub, x))):
        total = dot(a.get()[...], rows[0:half], TN) + dot(b.get()[...], rows[half:], TN)
        if i == 0:
            outs[1][...] = total.astype(BF)
            send(1)
        else:
            both.append(total.astype(BF))
    part = 128
    order_of = weave(2 * part)
    for first in range(0, both[0].shape[0], part):
        rows = jnp.concatenate([v[first : first + part] for v in both], axis=0)
        outs[0][2 * first : 2 * (first + part)] = dot(order_of, rows).astype(BF)
        send(0, 2 * first, 2 * (first + part))


def hot_kernel(ins, outs, send, x, c, w_in, w_out):
    parts, blocks = ins[0:8], ins[8:13]
    own, near, away = outs[0:3]
    grads = outs[3:7]
    mid = parts[0].target.shape[0] // 2
    units = blocks[0].target.shape[0] // 3
    count = 4 * units
    cut = blocks[3].target.shape[0]
    for b, (block, start) in enumerate(((0, 0), (1, 0), (2, 0), (3, 0), (4, cut))):
        ref = blocks[block].get()
        end = start + ref.shape[0]
        for kind in range(3):
            lo, hi = max(start, units * kind), min(end, units * kind + units)
            if lo < hi:
                target, base = (w_out, 0) if kind == 2 else (w_in, count * kind)
                base = base + units * min(b, 3) + lo - units * kind
                target[base : base + hi - lo] = ref[lo - start : hi - start]
    for i, part in enumerate(parts):
        part = part.get()
        x[mid * i : mid * i + mid] = part[0:mid]
        c[mid * i : mid * i + mid] = part[mid:]
    hs, ds = [], []
    step = 256
    for first in range(0, x.shape[0], step):
        r = slice(first, first + step)
        gu = dot(x[r], w_in[...], NT)
        dh = dot(c[r], w_out[...], NT)
        h, dg, du = gated(gu[:, 0:count], gu[:, count:], dh)
        hs.append(h)
        ds.append(jnp.concatenate([dg, du], axis=1))
    for first in range(0, x.shape[0], step):
        o = dot(hs[first // step], w_out[...]).astype(BF)
        dx = dot(ds[first // step], w_in[...]).astype(BF)
        for i in range(step // mid):
            part = first // mid + i
            s = slice(mid * i, mid * i + mid)
            ref, at = ((own, 0), (away, 0), (near, 0), (away, 256))[part // 2]
            at = at + 2 * mid * (part % 2)
            ref[at : at + mid] = o[s]
            ref[at + mid : at + 2 * mid] = dx[s]
    for i in (0, 1, 2):
        send(i)
    h, d = jnp.concatenate(hs, axis=0), jnp.concatenate(ds, axis=0)
    in_grad = dot(d, x[...], TN).astype(BF)
    out_grad = dot(h, c[...], TN).astype(BF)
    piece = grads[0].shape[1]
    for b in (3, 1, 2, 0):
        u = units * b
        for p in range(x.shape[1] // piece):
            cols = slice(piece * p, piece * p + piece)
            at = 3 * units * p
            grads[b][at : at + units] = in_grad[u : u + units, cols]
            grads[b][at + units : at + 2 * units] = in_grad[count + u : count + u + units, cols]
            grads[b][at + 2 * units : at + 3 * units] = out_grad[u : u + units, cols]
        send(3 + b)


def end_kernel(ins, outs, send):
    packed = ins[7]
    own, sibling, side_a, side_b, rw, ids, pick = [i.get() for i in ins[:7]]
    moe, grad = outs
    rows, width = moe.shape
    half = width // 2
    up, across = (lax.broadcasted_iota(jnp.int32, (rows, rows), d) for d in (0, 1))
    eye = up == across
    id_row = jnp.broadcast_to(ids[...], (rows, rows))
    id_col = as_column(id_row, eye)
    slot = jnp.sum(jnp.where((id_col == id_row) & (across < up), 1, 0), axis=1, keepdims=True)
    place = 8 * id_col + 2 * slot
    at = lax.broadcasted_iota(jnp.int32, (rows, packed.target.shape[0]), 1) - place
    scale = as_column(pick[...].astype(F32) * rw[1:2], eye)
    weight = as_column(rw[0:1], eye)
    mid = rows // 2
    cold = [None] * 4
    step = 256
    for first in range(0, packed.target.shape[0], step):
        here = packed.get(first + step)[first : first + step]
        for q in range(4):
            chosen = jnp.where(at[:, first : first + step] == 4 * (q // 2) + q % 2, 1.0, 0.0).astype(BF)
            term = dot(chosen, here)
            cold[q] = term if cold[q] is None else cold[q] + term
    for k in (0, 1):
        for f in (0, 1):
            cols = slice(half * f, half * f + half)
            for i, side in ((0, side_a), (1, side_b)):
                s = slice(mid * k, mid * k + mid)
                b = slice(rows * i + mid * k, rows * i + mid * k + mid)
                t = slice(mid * i, mid * i + mid)
                hot = own[b, cols].astype(F32) + sibling[b, cols].astype(F32) + side[s, cols].astype(F32)
                picked = cold[2 * k + f][t]
                if k == 0:
                    moe[t, cols] = (scale[t] * hot + weight[t] * picked).astype(BF)
                else:
                    grad[t, cols] = (hot + picked).astype(BF)
        send(k)


def per_device(tokens, cotangent, route_weight, cold_ids, hot_pick, hot_in, hot_out, cold_in, cold_out):
    rows, width = tokens.shape
    sizes = {name: lax.axis_size(name) for name in EVERY}
    nx, nz = sizes["x"], sizes["z"]
    units = hot_out.shape[0]
    experts = nx * sizes["l"] * nz * sizes["h"]
    cut = 80

    def along_x(value, step):
        return lax.ppermute(value, "x", [(i, (i + step) % nx) for i in range(nx)])

    def along_y(value, step):
        def index(y):
            return (y % 2) * 2 + y // 2

        return lax.ppermute(value, ("l", "h"), [(index(y), index((y + step) % 4)) for y in range(4)])

    def sibling(value):
        return lax.ppermute(value, "c", [(0, 1), (1, 0)])

    def exchange(value):
        return lax.all_to_all(value, EXPERTS, split_axis=0, concat_axis=0, tiled=True)

    pick_row = hot_pick.reshape(1, rows)
    id_row = cold_ids.reshape(1, rows)
    weight_rows = route_weight.T
    mid = width // 2
    piece = mid // nz
    h = lax.axis_index("h")
    gate_rows, up_rows, down_rows = cold_in[0, 0, :, 0], cold_in[0, 0, :, 1], cold_out[0, 0]

    block = jnp.concatenate([hot_in[:, 0], hot_in[:, 1], hot_out], axis=0)
    from_left, from_right = along_x(block, 1), along_x(block, -1)
    hot_a, hot_b = call(
        rows_kernel, [shape(rows, width)] * 2, [], 0, "rows",
        tokens, cotangent, weight_rows, pick_row,
    )
    side_a, side_b = along_y(hot_a, 1), along_y(hot_b, -1)
    near_a, near_b = sibling(hot_a), sibling(hot_b)
    far_a, far_b = along_x(from_left[:cut], 1), along_x(from_right[cut:], -1)
    parts = [hot_a, hot_b, near_a, near_b, side_a, side_b, sibling(side_a), sibling(side_b)]
    [packed] = call(
        send_kernel,
        [shape(experts * 8, mid)],
        [pltpu.VMEM((4 * rows, mid), BF)],
        2 * experts * 8 * 4 * rows * mid,
        "send",
        tokens, cotangent, weight_rows, id_row,
    )
    got = exchange(packed)

    grad_shape = shape(3 * units * 2 * nz, piece)
    own, near, away, grad_own, grad_left, grad_right, grad_far = call(
        hot_kernel,
        [shape(2 * rows, width), shape(2 * rows, width), shape(4 * rows, width)] + [grad_shape] * 4,
        [
            pltpu.VMEM((4 * rows, width), BF),
            pltpu.VMEM((4 * rows, width), BF),
            pltpu.VMEM((8 * units, width), BF),
            pltpu.VMEM((4 * units, width), BF),
        ],
        9 * 2 * 4 * rows * 4 * units * width,
        "hot",
        *parts, block, from_left, from_right, far_a, far_b,
    )
    part = grad_shape.shape[0] // 2

    def added(*terms):
        return sum(t.astype(F32) for t in terms).astype(BF)

    got_a, got_b = along_x(grad_far[:part], 1), along_x(grad_far[part:], -1)
    half_units = cold_out.shape[2]

    def cold(received, *after):
        picked = 2 * experts
        return call(
            cold_kernel,
            [shape(*received.shape)] + [shape(picked, half_units)] * 3,
            [pltpu.VMEM((picked, width), BF)] * 2,
            6 * 2 * picked * half_units * width,
            "cold",
            received, gate_rows, up_rows, down_rows, after=after,
        )

    got = gate(got, grad_far, gate_rows, up_rows)
    theirs = sibling(got)
    mine_back, *mine = cold(got)
    their_back, *their = cold(theirs, mine_back, got_a, got_b)
    came_back = sibling(their_back)
    [back] = call(
        add_kernel, [shape(*got.shape)], [], 0, "back", mine_back, came_back
    )
    to_right, to_left = call(
        mix_kernel, [grad_shape] * 2, [], 0, "mix",
        grad_right, grad_left, got_a, got_b, after=(back,),
    )
    got_right, got_left = along_x(to_right, 1), along_x(to_left, -1)
    returned = exchange(back)

    [total] = call(
        add_kernel, [grad_shape], [], 0, "total", grad_own, got_right, got_left
    )
    sent = lax.dynamic_slice_in_dim(total, (1 - h) * part, part, axis=0)
    kept = lax.dynamic_slice_in_dim(total, h * part, part, axis=0)
    came_half = lax.ppermute(sent, "h", [(0, 1), (1, 0)])
    away = sibling(away)
    summed = added(near, away[2 * rows :])
    hot_side_a, hot_side_b = along_y(summed[:rows], -1), along_y(summed[rows:], 1)
    in_grad, down_grad = call(
        cold_grad_kernel,
        [shape(2 * half_units, width), shape(half_units, width)],
        [pltpu.VMEM((4 * experts, width), BF)] * 2,
        3 * 2 * 4 * experts * half_units * width,
        "cold_grad",
        got, theirs, *mine, *their, after=(back,),
    )
    cold_in_grad = in_grad.reshape(1, 1, half_units, 2, width)
    cold_out_grad = down_grad[None, None]
    [total] = call(add_kernel, [shape(part, piece)], [], 0, "half", kept, came_half)
    total = gate(total, returned, cold_in_grad, hot_side_a, hot_side_b)
    shares = lax.all_to_all(total, "z", split_axis=0, concat_axis=0, tiled=True)
    moe_out, input_grad = call(
        end_kernel,
        [shape(rows, width), shape(rows, width)],
        [],
        2 * 4 * rows * 8 * experts * mid,
        "end",
        own, away, hot_side_a, hot_side_b, weight_rows, id_row, pick_row, returned,
    )
    [shares] = call(share_kernel, [shape(*shares.shape)], [], 0, "share", shares, after=(moe_out,))
    pieces = lax.all_to_all(shares, "z", split_axis=0, concat_axis=0, tiled=True)
    came = lax.ppermute(pieces, "h", [(0, 1), (1, 0)])
    hot_in_grad, hot_out_grad = call(
        assemble_kernel, [shape(2 * units, width), shape(units, width)], [], 0, "assemble",
        pieces, came, jnp.full((8, 128), h, jnp.int32),
    )
    hot_in_grad = hot_in_grad.reshape(units, 2, width)
    return moe_out, input_grad, hot_in_grad, hot_out_grad, cold_in_grad, cold_out_grad


def solution(mesh):
    fine = Mesh(mesh.devices.reshape(4, 2, 2, 8, 2), EVERY)
    loop, ep = ("x", "l", "c"), ("z", "h")
    tokens = P(EVERY, None)
    return jax.shard_map(
        per_device,
        mesh=fine,
        in_specs=(
            tokens, tokens, tokens, tokens, P(EVERY),
            P(loop, None, None), P(loop, None),
            P(loop, ep, None, None, None), P(loop, ep, None, None),
        ),
        out_specs=(
            tokens, tokens,
            P(loop, None, None), P(loop, None),
            P(loop, ep, None, None, None), P(loop, ep, None, None),
        ),
        check_vma=False,
    )
```

```python
import functools

import jax
import jax.numpy as jnp
from jax import lax
from jax.experimental import pallas as pl
from jax.experimental.pallas import tpu as pltpu
from jax.sharding import Mesh
from jax.sharding import PartitionSpec as P

BF = jnp.bfloat16
F32 = jnp.float32
NT = (((1,), (1,)), ((), ()))
TN = (((0,), (0,)), ((), ()))
EVERY = ("x", "l", "c", "z", "h")
EXPERTS = ("x", "l", "z", "h")


def dot(a, b, dims=(((1,), (0,)), ((), ()))):
    return lax.dot_general(a, b, dims, preferred_element_type=F32)


class Arriving:
    def __init__(self, source, target, semaphores, first, parts):
        self.target, self.rows = target, source.shape[0] // parts
        self.copies = [
            pltpu.make_async_copy(
                source.at[pl.ds(self.rows * i, self.rows)],
                target.at[pl.ds(self.rows * i, self.rows)],
                semaphores.at[first + i],
            )
            for i in range(parts)
        ]
        for copy in self.copies:
            copy.start()

    def get(self, upto=None):
        upto = self.target.shape[0] if upto is None else upto
        for i, copy in enumerate(self.copies):
            if copy is not None and self.rows * i < upto:
                copy.wait()
                self.copies[i] = None
        return self.target


def call(kernel, outs, scratch, flops, name, *args, after=()):
    moved = sum(a.size * a.dtype.itemsize for a in args)
    moved += sum(o.size * o.dtype.itemsize for o in outs)
    moved = moved if flops else 0
    n, m, skip, most = len(args), len(outs), len(after), 16
    parts = [4 if a.shape[0] == 1024 else 1 for a in args]

    def body(*refs):
        given, made = refs[:n], refs[n + skip : n + skip + m]
        held = refs[n + skip + m :]
        held_in, held_out, more = held[:n], held[n : n + m], held[n + m : -2]
        in_sem, out_sem = held[-2:]
        ins = [Arriving(given[i], held_in[i], in_sem, sum(parts[:i]), parts[i]) for i in range(n)]
        sent, begun = [], set()

        def send(i, lo=0, hi=None):
            begun.add(i)
            r = pl.ds(lo, (made[i].shape[0] if hi is None else hi) - lo)
            copy = pltpu.make_async_copy(held_out[i].at[r], made[i].at[r], out_sem.at[len(sent)])
            copy.start()
            sent.append(copy)

        kernel(ins, held_out, send, *more)
        for i in ins:
            i.get()
        for i in range(m):
            if i not in begun:
                send(i)
        for copy in sent:
            copy.wait()

    return pl.pallas_call(
        body,
        out_shape=outs,
        in_specs=[pl.BlockSpec(memory_space=pl.ANY)] * (n + skip),
        out_specs=[pl.BlockSpec(memory_space=pl.ANY)] * m,
        scratch_shapes=[pltpu.VMEM(a.shape, a.dtype) for a in args]
        + [pltpu.VMEM(o.shape, o.dtype) for o in outs]
        + list(scratch)
        + [pltpu.SemaphoreType.DMA((sum(parts),)), pltpu.SemaphoreType.DMA((most,))],
        compiler_params=pltpu.CompilerParams(vmem_limit_bytes=56 << 20),
        cost_estimate=pl.CostEstimate(flops=flops, bytes_accessed=moved, transcendentals=0),
        name=name,
    )(*args, *after)


def gate(value, *after):
    outside = pl.BlockSpec(memory_space=pl.ANY)
    return pl.pallas_call(
        lambda *refs: None,
        out_shape=jax.ShapeDtypeStruct(value.shape, value.dtype),
        in_specs=[outside] * (1 + len(after)),
        out_specs=outside,
        input_output_aliases={0: 0},
        name="gate",
    )(value, *after)


def shape(*dims):
    return jax.ShapeDtypeStruct(dims, BF)


def as_column(row, eye):
    return jnp.sum(jnp.where(eye, row, 0), axis=1, keepdims=True)


def eye_of(rows):
    up, across = (lax.broadcasted_iota(jnp.int32, (rows, rows), d) for d in (0, 1))
    return up == across


def rows_kernel(ins, outs, send):
    tok, cot, rw, pick = ins
    hot_a, hot_b = outs
    rows = hot_a.shape[0]
    mid = rows // 2
    tok = tok.get()
    hot_a[0:mid] = tok[0:mid]
    hot_b[0:mid] = tok[mid:rows]
    scale = as_column(pick.get()[...].astype(F32) * rw.get()[1:2], eye_of(rows))
    hot_cot = (scale * cot.get()[...].astype(F32)).astype(BF)
    hot_a[mid:rows] = hot_cot[0:mid]
    send(0)
    hot_b[mid:rows] = hot_cot[mid:rows]


def send_kernel(ins, outs, send, stack):
    tok, cot, rw, ids = [i.get() for i in ins]
    [packed] = outs
    rows, width = tok.shape
    half = width // 2
    up, across = (lax.broadcasted_iota(jnp.int32, (rows, rows), d) for d in (0, 1))
    eye = up == across
    id_row = jnp.broadcast_to(ids[...], (rows, rows))
    id_col = as_column(id_row, eye)
    slot_row = jnp.sum(
        jnp.where((id_col == id_row) & (up < across), 1, 0), axis=0, keepdims=True
    )
    place = 8 * ids[...] + 2 * slot_row
    cold_cot = (as_column(rw[0:1], eye) * cot[...].astype(F32)).astype(BF)
    stack[0:rows] = tok[:, 0:half]
    stack[rows : 2 * rows] = tok[:, half:width]
    stack[2 * rows : 3 * rows] = cold_cot[:, 0:half]
    stack[3 * rows : 4 * rows] = cold_cot[:, half:width]
    step = 256
    for first in range(0, packed.shape[0], step):
        at = first + lax.broadcasted_iota(jnp.int32, (step, rows), 0) - place
        pick_rows = jnp.concatenate(
            [jnp.where(at == 4 * k + f, 1.0, 0.0).astype(BF) for k in (0, 1) for f in (0, 1)], axis=1
        )
        packed[first : first + step] = dot(pick_rows, stack[...]).astype(BF)
        send(0, first, first + step)


def order(n, transposed):
    packed_at, plain_at = (
        lax.broadcasted_iota(jnp.int32, (n, n), d) for d in ((0, 1) if transposed else (1, 0))
    )
    sender, place = packed_at >> 3, packed_at & 7
    group = 2 * (place >> 2) + (place & 1)
    target = group * (n // 4) + 2 * sender + ((place >> 1) & 1)
    return jnp.where(plain_at == target, 1.0, 0.0).astype(BF)


def gated(g, u, dh):
    s = jax.nn.sigmoid(g)
    act = g * s
    h = (act * u).astype(BF)
    dg = (dh * u * (s * (1.0 + g * (1.0 - s)))).astype(BF)
    du = (dh * act).astype(BF)
    return h, dg, du


def unpack(packed, sort, x, c, first):
    n = sort.shape[0]
    quarter, half = n // 4, packed.target.shape[1]
    for j in range(packed.target.shape[0] // n):
        t = dot(sort, packed.get(n * j + n)[n * j : n * j + n]).astype(BF)
        r = slice(first + quarter * j, first + quarter * j + quarter)
        x[r, 0:half] = t[0:quarter]
        x[r, half:] = t[quarter : 2 * quarter]
        c[r, 0:half] = t[2 * quarter : 3 * quarter]
        c[r, half:] = t[3 * quarter :]


def cold_kernel(ins, outs, send, x, c):
    packed, wg, wu, wd = ins
    back, h_out, dg_out, du_out = outs
    n = 256
    quarter, half = n // 4, back.shape[1]
    unpack(packed, order(n, False), x, c, 0)
    wg = wg.get()
    g = dot(x[...], wg[...], NT)
    wu = wu.get()
    u = dot(x[...], wu[...], NT)
    wd = wd.get()
    dh = dot(c[...], wd[...], NT)
    h, dg, du = gated(g, u, dh)
    h_out[...] = h
    dg_out[...] = dg
    du_out[...] = du
    for i in (1, 2, 3):
        send(i)
    unsort = order(n, True)
    o = dot(h, wd[...]).astype(BF)
    dx = (dot(dg, wg[...]) + dot(du, wu[...])).astype(BF)
    for j in range(back.shape[0] // n):
        r = slice(quarter * j, quarter * j + quarter)
        t = jnp.concatenate([o[r, 0:half], o[r, half:], dx[r, 0:half], dx[r, half:]], axis=0)
        back[n * j : n * j + n] = dot(unsort, t).astype(BF)
        send(0, n * j, n * j + n)


def add_kernel(ins, outs, send):
    step = outs[0].shape[0] // 4
    for first in range(0, outs[0].shape[0], step):
        r = slice(first, first + step)
        outs[0][r] = sum(i.get(first + step)[r].astype(F32) for i in ins).astype(BF)
        send(0, first, first + step)


def mix_kernel(ins, outs, send):
    right, left, more_right, more_left = [i.get() for i in ins]
    part = more_right.shape[0]
    outs[0][0:part] = (right[0:part].astype(F32) + more_right[...].astype(F32)).astype(BF)
    outs[0][part:] = right[part:]
    send(0)
    outs[1][0:part] = left[0:part]
    outs[1][part:] = (left[part:].astype(F32) + more_left[...].astype(F32)).astype(BF)


def share_kernel(ins, outs, send):
    shares = ins[0].get()
    count = 8
    rows = shares.shape[0] // count
    total = sum(shares[rows * i : rows * i + rows].astype(F32) for i in range(count)).astype(BF)
    for i in range(count):
        outs[0][rows * i : rows * i + rows] = total


def weave(rows):
    row, column = (lax.broadcasted_iota(jnp.int32, (rows, rows), d) for d in (0, 1))
    return jnp.where(column == (row >> 1) + rows // 2 * (row & 1), 1.0, 0.0).astype(BF)


def assemble_kernel(ins, outs, send):
    mine, other, h = [i.get() for i in ins]
    inner, outer = outs
    units, width = outer.shape
    piece = mine.shape[1]
    count = mine.shape[0] // (3 * units)
    low = h[0:1] == 0
    order_of = weave(2 * units)
    for p in range(2 * count):
        at = 3 * units * (p % count)
        r = slice(at, at + 3 * units)
        a, b = mine[r].astype(F32), other[r].astype(F32)
        rows = jnp.where(low == (p < count), a, b).astype(BF)
        cols = slice(piece * p, piece * p + piece)
        inner[:, cols] = dot(order_of, rows[0 : 2 * units]).astype(BF)
        outer[:, cols] = rows[2 * units :]


def cold_grad_kernel(ins, outs, send, x, c):
    mine, theirs, ha, ga, ua, hb, gb, ub = ins
    sort = order(256, False)
    half = x.shape[0] // 2
    unpack(mine, sort, x, c, 0)
    unpack(theirs, sort, x, c, half)
    both = []
    for i, (a, b, rows) in enumerate(((ha, hb, c), (ga, gb, x), (ua, ub, x))):
        total = dot(a.get()[...], rows[0:half], TN) + dot(b.get()[...], rows[half:], TN)
        if i == 0:
            outs[1][...] = total.astype(BF)
            send(1)
        else:
            both.append(total.astype(BF))
    part = 128
    order_of = weave(2 * part)
    for first in range(0, both[0].shape[0], part):
        rows = jnp.concatenate([v[first : first + part] for v in both], axis=0)
        outs[0][2 * first : 2 * (first + part)] = dot(order_of, rows).astype(BF)
        send(0, 2 * first, 2 * (first + part))


def hot_kernel(ins, outs, send, x, c, w_in, w_out):
    parts, blocks = ins[0:8], ins[8:13]
    own, near, away = outs[0:3]
    grads, far = outs[3:6], outs[6:8]
    mid = parts[0].target.shape[0] // 2
    units = blocks[0].target.shape[0] // 3
    count = 4 * units
    cut = blocks[3].target.shape[0]
    for b, (block, start) in enumerate(((0, 0), (1, 0), (2, 0), (3, 0), (4, cut))):
        ref = blocks[block].get()
        end = start + ref.shape[0]
        for kind in range(3):
            lo, hi = max(start, units * kind), min(end, units * kind + units)
            if lo < hi:
                target, base = (w_out, 0) if kind == 2 else (w_in, count * kind)
                base = base + units * min(b, 3) + lo - units * kind
                target[base : base + hi - lo] = ref[lo - start : hi - start]
    for i, part in enumerate(parts):
        part = part.get()
        x[mid * i : mid * i + mid] = part[0:mid]
        c[mid * i : mid * i + mid] = part[mid:]
    hs, ds = [], []
    step = 256
    for first in range(0, x.shape[0], step):
        r = slice(first, first + step)
        gu = dot(x[r], w_in[...], NT)
        dh = dot(c[r], w_out[...], NT)
        h, dg, du = gated(gu[:, 0:count], gu[:, count:], dh)
        hs.append(h)
        ds.append(jnp.concatenate([dg, du], axis=1))
    for first in range(0, x.shape[0], step):
        o = dot(hs[first // step], w_out[...]).astype(BF)
        dx = dot(ds[first // step], w_in[...]).astype(BF)
        for i in range(step // mid):
            part = first // mid + i
            s = slice(mid * i, mid * i + mid)
            ref, at = ((own, 0), (away, 0), (near, 0), (away, 256))[part // 2]
            at = at + 2 * mid * (part % 2)
            ref[at : at + mid] = o[s]
            ref[at + mid : at + 2 * mid] = dx[s]
    for i in (0, 1, 2):
        send(i)
    h, d = jnp.concatenate(hs, axis=0), jnp.concatenate(ds, axis=0)
    in_grad = dot(d, x[...], TN).astype(BF)
    out_grad = dot(h, c[...], TN).astype(BF)
    piece = far[0].shape[1]
    for b in (3, 1, 2, 0):
        u = units * b
        pieces = x.shape[1] // piece
        for p in range(pieces):
            cols = slice(piece * p, piece * p + piece)
            to, at = (far[2 * p // pieces], p % (pieces // 2)) if b == 3 else (grads[b], p)
            at = 3 * units * at
            to[at : at + units] = in_grad[u : u + units, cols]
            to[at + units : at + 2 * units] = in_grad[count + u : count + u + units, cols]
            to[at + 2 * units : at + 3 * units] = out_grad[u : u + units, cols]
        if b == 3:
            send(6)
            send(7)
        else:
            send(3 + b)


def end_kernel(ins, outs, send):
    packed = ins[7]
    own, sibling, side_a, side_b, rw, ids, pick = [i.get() for i in ins[:7]]
    moe, grad = outs
    rows, width = moe.shape
    half = width // 2
    up, across = (lax.broadcasted_iota(jnp.int32, (rows, rows), d) for d in (0, 1))
    eye = up == across
    id_row = jnp.broadcast_to(ids[...], (rows, rows))
    id_col = as_column(id_row, eye)
    slot = jnp.sum(jnp.where((id_col == id_row) & (across < up), 1, 0), axis=1, keepdims=True)
    place = 8 * id_col + 2 * slot
    at = lax.broadcasted_iota(jnp.int32, (rows, packed.target.shape[0]), 1) - place
    scale = as_column(pick[...].astype(F32) * rw[1:2], eye)
    weight = as_column(rw[0:1], eye)
    mid = rows // 2
    cold = [None] * 4
    step = 256
    for first in range(0, packed.target.shape[0], step):
        here = packed.get(first + step)[first : first + step]
        for q in range(4):
            chosen = jnp.where(at[:, first : first + step] == 4 * (q // 2) + q % 2, 1.0, 0.0).astype(BF)
            term = dot(chosen, here)
            cold[q] = term if cold[q] is None else cold[q] + term
    for k in (0, 1):
        for f in (0, 1):
            cols = slice(half * f, half * f + half)
            for i, side in ((0, side_a), (1, side_b)):
                s = slice(mid * k, mid * k + mid)
                b = slice(rows * i + mid * k, rows * i + mid * k + mid)
                t = slice(mid * i, mid * i + mid)
                hot = own[b, cols].astype(F32) + sibling[b, cols].astype(F32) + side[s, cols].astype(F32)
                picked = cold[2 * k + f][t]
                if k == 0:
                    moe[t, cols] = (scale[t] * hot + weight[t] * picked).astype(BF)
                else:
                    grad[t, cols] = (hot + picked).astype(BF)
        send(k)


def per_device(tokens, cotangent, route_weight, cold_ids, hot_pick, hot_in, hot_out, cold_in, cold_out):
    rows, width = tokens.shape
    sizes = {name: lax.axis_size(name) for name in EVERY}
    nx, nz = sizes["x"], sizes["z"]
    units = hot_out.shape[0]
    experts = nx * sizes["l"] * nz * sizes["h"]
    cut = 80

    def along_x(value, step):
        return lax.ppermute(value, "x", [(i, (i + step) % nx) for i in range(nx)])

    def along_y(value, step):
        def index(y):
            return (y % 2) * 2 + y // 2

        return lax.ppermute(value, ("l", "h"), [(index(y), index((y + step) % 4)) for y in range(4)])

    def sibling(value):
        return lax.ppermute(value, "c", [(0, 1), (1, 0)])

    def exchange(value):
        return lax.all_to_all(value, EXPERTS, split_axis=0, concat_axis=0, tiled=True)

    pick_row = hot_pick.reshape(1, rows)
    id_row = cold_ids.reshape(1, rows)
    weight_rows = route_weight.T
    mid = width // 2
    piece = mid // nz
    h = lax.axis_index("h")
    gate_rows, up_rows, down_rows = cold_in[0, 0, :, 0], cold_in[0, 0, :, 1], cold_out[0, 0]

    block = jnp.concatenate([hot_in[:, 0], hot_in[:, 1], hot_out], axis=0)
    from_left, from_right = along_x(block, 1), along_x(block, -1)
    hot_a, hot_b = call(
        rows_kernel, [shape(rows, width)] * 2, [], 0, "rows",
        tokens, cotangent, weight_rows, pick_row,
    )
    side_a, side_b = along_y(hot_a, 1), along_y(hot_b, -1)
    near_a, near_b = sibling(hot_a), sibling(hot_b)
    far_a, far_b = along_x(from_left[:cut], 1), along_x(from_right[cut:], -1)
    parts = [hot_a, hot_b, near_a, near_b, side_a, side_b, sibling(side_a), sibling(side_b)]
    [packed] = call(
        send_kernel,
        [shape(experts * 8, mid)],
        [pltpu.VMEM((4 * rows, mid), BF)],
        2 * experts * 8 * 4 * rows * mid,
        "send",
        tokens, cotangent, weight_rows, id_row,
    )
    got = exchange(packed)

    grad_shape = shape(3 * units * 2 * nz, piece)
    own, near, away, grad_own, grad_left, grad_right, grad_far_a, grad_far_b = call(
        hot_kernel,
        [shape(2 * rows, width), shape(2 * rows, width), shape(4 * rows, width)]
        + [grad_shape] * 3
        + [shape(grad_shape.shape[0] // 2, piece)] * 2,
        [
            pltpu.VMEM((4 * rows, width), BF),
            pltpu.VMEM((4 * rows, width), BF),
            pltpu.VMEM((8 * units, width), BF),
            pltpu.VMEM((4 * units, width), BF),
        ],
        1 << 36,
        "hot",
        *parts, block, from_left, from_right, far_a, far_b,
    )
    part = grad_shape.shape[0] // 2

    def added(*terms):
        return sum(t.astype(F32) for t in terms).astype(BF)

    got_a, got_b = along_x(grad_far_a, 1), along_x(grad_far_b, -1)
    half_units = cold_out.shape[2]

    def cold(received, *after):
        picked = 2 * experts
        return call(
            cold_kernel,
            [shape(*received.shape)] + [shape(picked, half_units)] * 3,
            [pltpu.VMEM((picked, width), BF)] * 2,
            6 * 2 * picked * half_units * width,
            "cold",
            received, gate_rows, up_rows, down_rows, after=after,
        )

    got = gate(got, grad_far_a, gate_rows, up_rows)
    theirs = sibling(got)
    mine_back, *mine = cold(got)
    their_back, *their = cold(theirs, mine_back, got_a, got_b)
    came_back = sibling(their_back)
    [back] = call(
        add_kernel, [shape(*got.shape)], [], 0, "back", mine_back, came_back
    )
    to_right, to_left = call(
        mix_kernel, [grad_shape] * 2, [], 0, "mix",
        grad_right, grad_left, got_a, got_b, after=(back,),
    )
    got_right, got_left = along_x(to_right, 1), along_x(to_left, -1)
    returned = exchange(back)

    away = sibling(away)
    summed = added(near, away[2 * rows :])
    hot_side_a, hot_side_b = along_y(summed[:rows], -1), along_y(summed[rows:], 1)
    in_grad, down_grad = call(
        cold_grad_kernel,
        [shape(2 * half_units, width), shape(half_units, width)],
        [pltpu.VMEM((4 * experts, width), BF)] * 2,
        3 * 2 * 4 * experts * half_units * width,
        "cold_grad",
        got, theirs, *mine, *their, after=(back,),
    )
    cold_in_grad = in_grad.reshape(1, 1, half_units, 2, width)
    cold_out_grad = down_grad[None, None]
    [total] = call(
        add_kernel, [grad_shape], [], 0, "total", grad_own, got_right, got_left, after=(down_grad,)
    )
    sent = lax.dynamic_slice_in_dim(total, (1 - h) * part, part, axis=0)
    kept = lax.dynamic_slice_in_dim(total, h * part, part, axis=0)
    came_half = lax.ppermute(sent, "h", [(0, 1), (1, 0)])
    [total] = call(add_kernel, [shape(part, piece)], [], 0, "half", kept, came_half)
    total = gate(total, returned, cold_in_grad, hot_side_a, hot_side_b)
    shares = lax.all_to_all(total, "z", split_axis=0, concat_axis=0, tiled=True)
    moe_out, input_grad = call(
        end_kernel,
        [shape(rows, width), shape(rows, width)],
        [],
        2 * 4 * rows * 8 * experts * mid,
        "end",
        own, away, hot_side_a, hot_side_b, weight_rows, id_row, pick_row, returned,
    )
    [shares] = call(share_kernel, [shape(*shares.shape)], [], 0, "share", shares, after=(moe_out,))
    pieces = lax.all_to_all(shares, "z", split_axis=0, concat_axis=0, tiled=True)
    came = lax.ppermute(pieces, "h", [(0, 1), (1, 0)])
    hot_in_grad, hot_out_grad = call(
        assemble_kernel, [shape(2 * units, width), shape(units, width)], [], 0, "assemble",
        pieces, came, jnp.full((8, 128), h, jnp.int32),
    )
    hot_in_grad = hot_in_grad.reshape(units, 2, width)
    return moe_out, input_grad, hot_in_grad, hot_out_grad, cold_in_grad, cold_out_grad


def solution(mesh):
    fine = Mesh(mesh.devices.reshape(4, 2, 2, 8, 2), EVERY)
    loop, ep = ("x", "l", "c"), ("z", "h")
    tokens = P(EVERY, None)
    return jax.shard_map(
        per_device,
        mesh=fine,
        in_specs=(
            tokens, tokens, tokens, tokens, P(EVERY),
            P(loop, None, None), P(loop, None),
            P(loop, ep, None, None, None), P(loop, ep, None, None),
        ),
        out_specs=(
            tokens, tokens,
            P(loop, None, None), P(loop, None),
            P(loop, ep, None, None, None), P(loop, ep, None, None),
        ),
        check_vma=False,
    )
```

```python
import functools

import jax
import jax.numpy as jnp
from jax import lax
from jax.experimental import pallas as pl
from jax.experimental.pallas import tpu as pltpu
from jax.sharding import Mesh
from jax.sharding import PartitionSpec as P

BF = jnp.bfloat16
F32 = jnp.float32
NT = (((1,), (1,)), ((), ()))
TN = (((0,), (0,)), ((), ()))
EVERY = ("x", "l", "c", "z", "h")
EXPERTS = ("x", "l", "z", "h")


def dot(a, b, dims=(((1,), (0,)), ((), ()))):
    return lax.dot_general(a, b, dims, preferred_element_type=F32)


class Arriving:
    def __init__(self, source, target, semaphores, first, parts):
        self.target, self.rows = target, source.shape[0] // parts
        self.copies = [
            pltpu.make_async_copy(
                source.at[pl.ds(self.rows * i, self.rows)],
                target.at[pl.ds(self.rows * i, self.rows)],
                semaphores.at[first + i],
            )
            for i in range(parts)
        ]
        for copy in self.copies:
            copy.start()

    def get(self, upto=None):
        upto = self.target.shape[0] if upto is None else upto
        for i, copy in enumerate(self.copies):
            if copy is not None and self.rows * i < upto:
                copy.wait()
                self.copies[i] = None
        return self.target


def call(kernel, outs, scratch, flops, name, *args, after=()):
    moved = sum(a.size * a.dtype.itemsize for a in args)
    moved += sum(o.size * o.dtype.itemsize for o in outs)
    moved = moved if flops else 0
    n, m, skip, most = len(args), len(outs), len(after), 16
    parts = [4 if a.shape[0] == 1024 else 1 for a in args]

    def body(*refs):
        given, made = refs[:n], refs[n + skip : n + skip + m]
        held = refs[n + skip + m :]
        held_in, held_out, more = held[:n], held[n : n + m], held[n + m : -2]
        in_sem, out_sem = held[-2:]
        ins = [Arriving(given[i], held_in[i], in_sem, sum(parts[:i]), parts[i]) for i in range(n)]
        sent, begun = [], set()

        def send(i, lo=0, hi=None):
            begun.add(i)
            r = pl.ds(lo, (made[i].shape[0] if hi is None else hi) - lo)
            copy = pltpu.make_async_copy(held_out[i].at[r], made[i].at[r], out_sem.at[len(sent)])
            copy.start()
            sent.append(copy)

        kernel(ins, held_out, send, *more)
        for i in ins:
            i.get()
        for i in range(m):
            if i not in begun:
                send(i)
        for copy in sent:
            copy.wait()

    return pl.pallas_call(
        body,
        out_shape=outs,
        in_specs=[pl.BlockSpec(memory_space=pl.ANY)] * (n + skip),
        out_specs=[pl.BlockSpec(memory_space=pl.ANY)] * m,
        scratch_shapes=[pltpu.VMEM(a.shape, a.dtype) for a in args]
        + [pltpu.VMEM(o.shape, o.dtype) for o in outs]
        + list(scratch)
        + [pltpu.SemaphoreType.DMA((sum(parts),)), pltpu.SemaphoreType.DMA((most,))],
        compiler_params=pltpu.CompilerParams(vmem_limit_bytes=56 << 20),
        cost_estimate=pl.CostEstimate(flops=flops, bytes_accessed=moved, transcendentals=0),
        name=name,
    )(*args, *after)


def gate(value, *after):
    outside = pl.BlockSpec(memory_space=pl.ANY)
    return pl.pallas_call(
        lambda *refs: None,
        out_shape=jax.ShapeDtypeStruct(value.shape, value.dtype),
        in_specs=[outside] * (1 + len(after)),
        out_specs=outside,
        input_output_aliases={0: 0},
        name="gate",
    )(value, *after)


def shape(*dims):
    return jax.ShapeDtypeStruct(dims, BF)


def as_column(row, eye):
    return jnp.sum(jnp.where(eye, row, 0), axis=1, keepdims=True)


def eye_of(rows):
    up, across = (lax.broadcasted_iota(jnp.int32, (rows, rows), d) for d in (0, 1))
    return up == across


def rows_kernel(ins, outs, send):
    tok, cot, rw, pick = ins
    hot_a, hot_b = outs
    rows = hot_a.shape[0]
    mid = rows // 2
    tok = tok.get()
    hot_a[0:mid] = tok[0:mid]
    hot_b[0:mid] = tok[mid:rows]
    scale = as_column(pick.get()[...].astype(F32) * rw.get()[1:2], eye_of(rows))
    hot_cot = (scale * cot.get()[...].astype(F32)).astype(BF)
    hot_a[mid:rows] = hot_cot[0:mid]
    send(0)
    hot_b[mid:rows] = hot_cot[mid:rows]


def send_kernel(ins, outs, send, stack):
    tok, cot, rw, ids = [i.get() for i in ins]
    [packed] = outs
    rows, width = tok.shape
    half = width // 2
    up, across = (lax.broadcasted_iota(jnp.int32, (rows, rows), d) for d in (0, 1))
    eye = up == across
    id_row = jnp.broadcast_to(ids[...], (rows, rows))
    id_col = as_column(id_row, eye)
    slot_row = jnp.sum(
        jnp.where((id_col == id_row) & (up < across), 1, 0), axis=0, keepdims=True
    )
    place = 8 * ids[...] + 2 * slot_row
    cold_cot = (as_column(rw[0:1], eye) * cot[...].astype(F32)).astype(BF)
    stack[0:rows] = tok[:, 0:half]
    stack[rows : 2 * rows] = tok[:, half:width]
    stack[2 * rows : 3 * rows] = cold_cot[:, 0:half]
    stack[3 * rows : 4 * rows] = cold_cot[:, half:width]
    step = 256
    for first in range(0, packed.shape[0], step):
        at = first + lax.broadcasted_iota(jnp.int32, (step, rows), 0) - place
        pick_rows = jnp.concatenate(
            [jnp.where(at == 4 * k + f, 1.0, 0.0).astype(BF) for k in (0, 1) for f in (0, 1)], axis=1
        )
        packed[first : first + step] = dot(pick_rows, stack[...]).astype(BF)
        send(0, first, first + step)


def order(n, transposed):
    packed_at, plain_at = (
        lax.broadcasted_iota(jnp.int32, (n, n), d) for d in ((0, 1) if transposed else (1, 0))
    )
    sender, place = packed_at >> 3, packed_at & 7
    group = 2 * (place >> 2) + (place & 1)
    target = group * (n // 4) + 2 * sender + ((place >> 1) & 1)
    return jnp.where(plain_at == target, 1.0, 0.0).astype(BF)


def gated(g, u, dh):
    s = jax.nn.sigmoid(g)
    act = g * s
    h = (act * u).astype(BF)
    dg = (dh * u * (s * (1.0 + g * (1.0 - s)))).astype(BF)
    du = (dh * act).astype(BF)
    return h, dg, du


def unpack(packed, sort, x, c, first):
    n = sort.shape[0]
    quarter, half = n // 4, packed.target.shape[1]
    for j in range(packed.target.shape[0] // n):
        t = dot(sort, packed.get(n * j + n)[n * j : n * j + n]).astype(BF)
        r = slice(first + quarter * j, first + quarter * j + quarter)
        x[r, 0:half] = t[0:quarter]
        x[r, half:] = t[quarter : 2 * quarter]
        c[r, 0:half] = t[2 * quarter : 3 * quarter]
        c[r, half:] = t[3 * quarter :]


def cold_kernel(ins, outs, send, x, c):
    packed, wg, wu, wd = ins
    back, h_out, dg_out, du_out = outs
    n = 256
    quarter, half = n // 4, back.shape[1]
    unpack(packed, order(n, False), x, c, 0)
    wg = wg.get()
    g = dot(x[...], wg[...], NT)
    wu = wu.get()
    u = dot(x[...], wu[...], NT)
    wd = wd.get()
    dh = dot(c[...], wd[...], NT)
    h, dg, du = gated(g, u, dh)
    h_out[...] = h
    dg_out[...] = dg
    du_out[...] = du
    for i in (1, 2, 3):
        send(i)
    unsort = order(n, True)
    o = dot(h, wd[...]).astype(BF)
    dx = (dot(dg, wg[...]) + dot(du, wu[...])).astype(BF)
    for j in range(back.shape[0] // n):
        r = slice(quarter * j, quarter * j + quarter)
        t = jnp.concatenate([o[r, 0:half], o[r, half:], dx[r, 0:half], dx[r, half:]], axis=0)
        back[n * j : n * j + n] = dot(unsort, t).astype(BF)
        send(0, n * j, n * j + n)


def add_kernel(ins, outs, send):
    step = outs[0].shape[0] // 4
    for first in range(0, outs[0].shape[0], step):
        r = slice(first, first + step)
        outs[0][r] = sum(i.get(first + step)[r].astype(F32) for i in ins).astype(BF)
        send(0, first, first + step)


def mix_kernel(ins, outs, send):
    right, left, more_right, more_left = [i.get() for i in ins]
    part = more_right.shape[0]
    outs[0][0:part] = (right[0:part].astype(F32) + more_right[...].astype(F32)).astype(BF)
    outs[0][part:] = right[part:]
    send(0)
    outs[1][0:part] = left[0:part]
    outs[1][part:] = (left[part:].astype(F32) + more_left[...].astype(F32)).astype(BF)


def share_kernel(ins, outs, send):
    shares = ins[0].get()
    count = 8
    rows = shares.shape[0] // count
    total = sum(shares[rows * i : rows * i + rows].astype(F32) for i in range(count)).astype(BF)
    for i in range(count):
        outs[0][rows * i : rows * i + rows] = total


def weave(rows):
    row, column = (lax.broadcasted_iota(jnp.int32, (rows, rows), d) for d in (0, 1))
    return jnp.where(column == (row >> 1) + rows // 2 * (row & 1), 1.0, 0.0).astype(BF)


def assemble_kernel(ins, outs, send):
    mine, other, h = [i.get() for i in ins]
    inner, outer = outs
    units, width = outer.shape
    piece = mine.shape[1]
    count = mine.shape[0] // (3 * units)
    low = h[0:1] == 0
    order_of = weave(2 * units)
    for p in range(2 * count):
        at = 3 * units * (p % count)
        r = slice(at, at + 3 * units)
        a, b = mine[r].astype(F32), other[r].astype(F32)
        rows = jnp.where(low == (p < count), a, b).astype(BF)
        cols = slice(piece * p, piece * p + piece)
        inner[:, cols] = dot(order_of, rows[0 : 2 * units]).astype(BF)
        outer[:, cols] = rows[2 * units :]


def cold_grad_kernel(ins, outs, send, x, c):
    mine, theirs, ha, ga, ua, hb, gb, ub = ins
    sort = order(256, False)
    half = x.shape[0] // 2
    unpack(mine, sort, x, c, 0)
    unpack(theirs, sort, x, c, half)
    both = []
    for i, (a, b, rows) in enumerate(((ha, hb, c), (ga, gb, x), (ua, ub, x))):
        total = dot(a.get()[...], rows[0:half], TN) + dot(b.get()[...], rows[half:], TN)
        if i == 0:
            outs[1][...] = total.astype(BF)
            send(1)
        else:
            both.append(total.astype(BF))
    part = 128
    order_of = weave(2 * part)
    for first in range(0, both[0].shape[0], part):
        rows = jnp.concatenate([v[first : first + part] for v in both], axis=0)
        outs[0][2 * first : 2 * (first + part)] = dot(order_of, rows).astype(BF)
        send(0, 2 * first, 2 * (first + part))


def hot_kernel(ins, outs, send, x, c, w_in, w_out):
    parts, blocks = ins[0:8], ins[8:13]
    own, near, away = outs[0:3]
    grads, far = outs[3:6], outs[6:8]
    mid = parts[0].target.shape[0] // 2
    units = blocks[0].target.shape[0] // 3
    count = 4 * units
    cut = blocks[3].target.shape[0]
    for b, (block, start) in enumerate(((0, 0), (1, 0), (2, 0), (3, 0), (4, cut))):
        ref = blocks[block].get()
        end = start + ref.shape[0]
        for kind in range(3):
            lo, hi = max(start, units * kind), min(end, units * kind + units)
            if lo < hi:
                target, base = (w_out, 0) if kind == 2 else (w_in, count * kind)
                base = base + units * min(b, 3) + lo - units * kind
                target[base : base + hi - lo] = ref[lo - start : hi - start]
    for i, part in enumerate(parts):
        part = part.get()
        x[mid * i : mid * i + mid] = part[0:mid]
        c[mid * i : mid * i + mid] = part[mid:]
    hs, ds = [], []
    step = 256
    for first in range(0, x.shape[0], step):
        r = slice(first, first + step)
        gu = dot(x[r], w_in[...], NT)
        dh = dot(c[r], w_out[...], NT)
        h, dg, du = gated(gu[:, 0:count], gu[:, count:], dh)
        hs.append(h)
        ds.append(jnp.concatenate([dg, du], axis=1))
    for first in range(0, x.shape[0], step):
        o = dot(hs[first // step], w_out[...]).astype(BF)
        dx = dot(ds[first // step], w_in[...]).astype(BF)
        for i in range(step // mid):
            part = first // mid + i
            s = slice(mid * i, mid * i + mid)
            ref, at = ((own, 0), (away, 0), (near, 0), (away, 256))[part // 2]
            at = at + 2 * mid * (part % 2)
            ref[at : at + mid] = o[s]
            ref[at + mid : at + 2 * mid] = dx[s]
    for i in (0, 1, 2):
        send(i)
    h, d = jnp.concatenate(hs, axis=0), jnp.concatenate(ds, axis=0)
    in_grad = dot(d, x[...], TN).astype(BF)
    out_grad = dot(h, c[...], TN).astype(BF)
    piece = far[0].shape[1]
    for b in (3, 1, 2, 0):
        u = units * b
        pieces = x.shape[1] // piece
        for p in range(pieces):
            cols = slice(piece * p, piece * p + piece)
            to, at = (far[2 * p // pieces], p % (pieces // 2)) if b == 3 else (grads[b], p)
            at = 3 * units * at
            to[at : at + units] = in_grad[u : u + units, cols]
            to[at + units : at + 2 * units] = in_grad[count + u : count + u + units, cols]
            to[at + 2 * units : at + 3 * units] = out_grad[u : u + units, cols]
        if b == 3:
            send(6)
            send(7)
        else:
            send(3 + b)


def end_kernel(ins, outs, send):
    packed = ins[7]
    own, sibling, side_a, side_b, rw, ids, pick = [i.get() for i in ins[:7]]
    moe, grad = outs
    rows, width = moe.shape
    half = width // 2
    up, across = (lax.broadcasted_iota(jnp.int32, (rows, rows), d) for d in (0, 1))
    eye = up == across
    id_row = jnp.broadcast_to(ids[...], (rows, rows))
    id_col = as_column(id_row, eye)
    slot = jnp.sum(jnp.where((id_col == id_row) & (across < up), 1, 0), axis=1, keepdims=True)
    place = 8 * id_col + 2 * slot
    at = lax.broadcasted_iota(jnp.int32, (rows, packed.target.shape[0]), 1) - place
    scale = as_column(pick[...].astype(F32) * rw[1:2], eye)
    weight = as_column(rw[0:1], eye)
    mid = rows // 2
    cold = [None] * 4
    step = 256
    for first in range(0, packed.target.shape[0], step):
        here = packed.get(first + step)[first : first + step]
        for q in range(4):
            chosen = jnp.where(at[:, first : first + step] == 4 * (q // 2) + q % 2, 1.0, 0.0).astype(BF)
            term = dot(chosen, here)
            cold[q] = term if cold[q] is None else cold[q] + term
    for k in (0, 1):
        for f in (0, 1):
            cols = slice(half * f, half * f + half)
            for i, side in ((0, side_a), (1, side_b)):
                s = slice(mid * k, mid * k + mid)
                b = slice(rows * i + mid * k, rows * i + mid * k + mid)
                t = slice(mid * i, mid * i + mid)
                hot = own[b, cols].astype(F32) + sibling[b, cols].astype(F32) + side[s, cols].astype(F32)
                picked = cold[2 * k + f][t]
                if k == 0:
                    moe[t, cols] = (scale[t] * hot + weight[t] * picked).astype(BF)
                else:
                    grad[t, cols] = (hot + picked).astype(BF)
        send(k)


def per_device(tokens, cotangent, route_weight, cold_ids, hot_pick, hot_in, hot_out, cold_in, cold_out):
    rows, width = tokens.shape
    sizes = {name: lax.axis_size(name) for name in EVERY}
    nx, nz = sizes["x"], sizes["z"]
    units = hot_out.shape[0]
    experts = nx * sizes["l"] * nz * sizes["h"]
    cut = 80

    def along_x(value, step):
        return lax.ppermute(value, "x", [(i, (i + step) % nx) for i in range(nx)])

    def along_y(value, step):
        def index(y):
            return (y % 2) * 2 + y // 2

        return lax.ppermute(value, ("l", "h"), [(index(y), index((y + step) % 4)) for y in range(4)])

    def sibling(value):
        return lax.ppermute(value, "c", [(0, 1), (1, 0)])

    def exchange(value):
        return lax.all_to_all(value, EXPERTS, split_axis=0, concat_axis=0, tiled=True)

    pick_row = hot_pick.reshape(1, rows)
    id_row = cold_ids.reshape(1, rows)
    weight_rows = route_weight.T
    mid = width // 2
    piece = mid // nz
    h = lax.axis_index("h")
    gate_rows, up_rows, down_rows = cold_in[0, 0, :, 0], cold_in[0, 0, :, 1], cold_out[0, 0]

    block = jnp.concatenate([hot_in[:, 0], hot_in[:, 1], hot_out], axis=0)
    from_left, from_right = along_x(block, 1), along_x(block, -1)
    hot_a, hot_b = call(
        rows_kernel, [shape(rows, width)] * 2, [], 0, "rows",
        tokens, cotangent, weight_rows, pick_row,
    )
    side_a, side_b = along_y(hot_a, 1), along_y(hot_b, -1)
    near_a, near_b = sibling(hot_a), sibling(hot_b)
    far_a, far_b = along_x(from_left[:cut], 1), along_x(from_right[cut:], -1)
    parts = [hot_a, hot_b, near_a, near_b, side_a, side_b, sibling(side_a), sibling(side_b)]
    [packed] = call(
        send_kernel,
        [shape(experts * 8, mid)],
        [pltpu.VMEM((4 * rows, mid), BF)],
        2 * experts * 8 * 4 * rows * mid,
        "send",
        tokens, cotangent, weight_rows, id_row,
    )
    got = exchange(packed)

    grad_shape = shape(3 * units * 2 * nz, piece)
    own, near, away, grad_own, grad_left, grad_right, grad_far_a, grad_far_b = call(
        hot_kernel,
        [shape(2 * rows, width), shape(2 * rows, width), shape(4 * rows, width)]
        + [grad_shape] * 3
        + [shape(grad_shape.shape[0] // 2, piece)] * 2,
        [
            pltpu.VMEM((4 * rows, width), BF),
            pltpu.VMEM((4 * rows, width), BF),
            pltpu.VMEM((8 * units, width), BF),
            pltpu.VMEM((4 * units, width), BF),
        ],
        1 << 36,
        "hot",
        *parts, block, from_left, from_right, far_a, far_b,
    )
    part = grad_shape.shape[0] // 2

    def added(*terms):
        return sum(t.astype(F32) for t in terms).astype(BF)

    got_a, got_b = along_x(grad_far_a, 1), along_x(grad_far_b, -1)
    half_units = cold_out.shape[2]

    def cold(received, *after):
        picked = 2 * experts
        return call(
            cold_kernel,
            [shape(*received.shape)] + [shape(picked, half_units)] * 3,
            [pltpu.VMEM((picked, width), BF)] * 2,
            6 * 2 * picked * half_units * width,
            "cold",
            received, gate_rows, up_rows, down_rows, after=after,
        )

    to_right, to_left = call(
        mix_kernel, [grad_shape] * 2, [], 0, "mix",
        grad_right, grad_left, got_a, got_b,
    )
    got_right, got_left = along_x(to_right, 1), along_x(to_left, -1)
    got = gate(got, to_right, to_left, gate_rows, up_rows)
    theirs = sibling(got)
    mine_back, *mine = cold(got)
    their_back, *their = cold(theirs, mine_back)
    came_back = sibling(their_back)
    [back] = call(
        add_kernel, [shape(*got.shape)], [], 0, "back", mine_back, came_back,
    )
    returned = exchange(back)

    away = sibling(away)
    summed = added(near, away[2 * rows :])
    hot_side_a, hot_side_b = along_y(summed[:rows], -1), along_y(summed[rows:], 1)
    in_grad, down_grad = call(
        cold_grad_kernel,
        [shape(2 * half_units, width), shape(half_units, width)],
        [pltpu.VMEM((4 * experts, width), BF)] * 2,
        3 * 2 * 4 * experts * half_units * width,
        "cold_grad",
        got, theirs, *mine, *their, after=(back,),
    )
    cold_in_grad = in_grad.reshape(1, 1, half_units, 2, width)
    cold_out_grad = down_grad[None, None]
    [total] = call(
        add_kernel, [grad_shape], [], 0, "total", grad_own, got_right, got_left, after=(down_grad,)
    )
    sent = lax.dynamic_slice_in_dim(total, (1 - h) * part, part, axis=0)
    kept = lax.dynamic_slice_in_dim(total, h * part, part, axis=0)
    came_half = lax.ppermute(sent, "h", [(0, 1), (1, 0)])
    [total] = call(add_kernel, [shape(part, piece)], [], 0, "half", kept, came_half)
    total = gate(total, returned, cold_in_grad, hot_side_a, hot_side_b)
    shares = lax.all_to_all(total, "z", split_axis=0, concat_axis=0, tiled=True)
    moe_out, input_grad = call(
        end_kernel,
        [shape(rows, width), shape(rows, width)],
        [],
        2 * 4 * rows * 8 * experts * mid,
        "end",
        own, away, hot_side_a, hot_side_b, weight_rows, id_row, pick_row, returned,
    )
    [shares] = call(share_kernel, [shape(*shares.shape)], [], 0, "share", shares, after=(moe_out,))
    pieces = lax.all_to_all(shares, "z", split_axis=0, concat_axis=0, tiled=True)
    came = lax.ppermute(pieces, "h", [(0, 1), (1, 0)])
    hot_in_grad, hot_out_grad = call(
        assemble_kernel, [shape(2 * units, width), shape(units, width)], [], 0, "assemble",
        pieces, came, jnp.full((8, 128), h, jnp.int32),
    )
    hot_in_grad = hot_in_grad.reshape(units, 2, width)
    return moe_out, input_grad, hot_in_grad, hot_out_grad, cold_in_grad, cold_out_grad


def solution(mesh):
    fine = Mesh(mesh.devices.reshape(4, 2, 2, 8, 2), EVERY)
    loop, ep = ("x", "l", "c"), ("z", "h")
    tokens = P(EVERY, None)
    return jax.shard_map(
        per_device,
        mesh=fine,
        in_specs=(
            tokens, tokens, tokens, tokens, P(EVERY),
            P(loop, None, None), P(loop, None),
            P(loop, ep, None, None, None), P(loop, ep, None, None),
        ),
        out_specs=(
            tokens, tokens,
            P(loop, None, None), P(loop, None),
            P(loop, ep, None, None, None), P(loop, ep, None, None),
        ),
        check_vma=False,
    )
```
